128 devices in a mesh: morton: 32 (over z, x, core), chan: 4 (over y).
Axes of the slice: x: 4, y: 4, z: 4, core: 2. Of those that a mesh axis runs over, the one named last changes fastest.
Arguments:
- pressure: bfloat16 [256, 524288], P('chan', 'morton'), may hold values from -6 to 6
- cotangent: bfloat16 [256, 524288], P('chan', 'morton'), may hold values from -8 to 8
- fluid_mask: int32 [524288], P('morton'), may hold values 0 or 1
- weight: bfloat16 [256, 512], replicated, may hold values from -0.25 to 0.25
Outputs:
- grad_pressure: float32 [256, 524288], P('chan', 'morton')
- grad_weight: float32 [256, 512], P('chan', 'morton')
The draws below stay inside these ranges and needn't reach their ends.
All inputs are finite; a program needn't handle non-finite values. No bound on the sum of `fluid_mask` on one device may be relied on, other than what follows from the above.
Results may differ from the reference program's by a relative error of at most 0.02.
Values may be sent and summed in bfloat16 or wider, within the bound.
No kernel may reach another device: no remote copies, remote signals or barrier semaphores. Data moves between devices by JAX's collectives and lax.ppermute only.
A program may use at most 192 MiB of HBM per device.

```python
import jax
import jax.numpy as jnp
from jax import lax

C = 256
LEAF_DEV = 16384
LEAVES = 524288
N_MORTON = 32


def draw_cotangent(key, part):
    key = jax.random.fold_in(key, 11)
    subkeys = jax.random.split(key, 5)
    values = jax.random.normal(subkeys[0], (C, LEAVES), jnp.float32)
    run_lengths = (max(LEAF_DEV // 16, 1), LEAF_DEV, min(4 * LEAF_DEV, LEAVES))
    for draw_index in range(3):
        run_length = run_lengths[draw_index]
        offsets = 0.7 * jax.random.normal(subkeys[draw_index + 1], (C, LEAVES // run_length), jnp.float32)
        values = values + jnp.repeat(offsets, run_length, axis=1, total_repeat_length=LEAVES)
    return jnp.clip(values, -8.0, 8.0).astype(jnp.bfloat16)


def touch_ends(values, stream_key, least, high):
    longest = values.shape.index(max(values.shape))
    spots = []
    for shift in (0, 1):
        where = [jax.random.randint(jax.random.fold_in(stream_key, axis), (), 0, length) for axis, length in enumerate(values.shape)]
        where[longest] = (where[longest] + shift) % values.shape[longest]
        spots.append(tuple(where))
    return values.at[spots[0]].set(least).at[spots[1]].set(high)


def levels(key, dims, pieces, smallest, high):
    def one(axis_at, parts):
        draws = jax.random.uniform(jax.random.fold_in(jax.random.fold_in(key, 6), axis_at), (parts,), jnp.float32, smallest / len(pieces), high / len(pieces))
        return jnp.repeat(jnp.exp(draws), dims[axis_at] // parts).reshape((-1,) + (1,) * (len(dims) - axis_at - 1))

    level = one(*pieces[0])
    for cut in pieces[1:]:
        level = level * one(*cut)
    return level


def scatter_about(stream_key, shape, scale, limit, shards=(), held_as=jnp.bfloat16):
    array = jax.random.normal(stream_key, shape, jnp.float32) * scale
    if len(shards) > 0:
        array = levels(stream_key, shape, shards, -0.22, 0.18) * array
    return jnp.clip(array, min=-limit, max=limit).astype(held_as)


def setup_inputs(seed: int = 0) -> dict:
    splits = jax.random.split(jax.random.key(seed), 5)
    return {
        "pressure": scatter_about(splits[0], (C, LEAVES), 1.0, 6.0, ((0, 4), (1, 32))),
        "cotangent": draw_cotangent(jax.random.fold_in(splits[4], 71), 0),
        "fluid_mask": touch_ends((jax.random.randint(splits[2], (LEAVES,), 0, 4) < 3).astype(jnp.int32), jax.random.fold_in(splits[2], 1), 0, 1),
        "weight": scatter_about(splits[3], (C, 2 * C), (2 * C) ** -0.5, 0.25),
    }


half_root = 0.7071067811865476
inv_root_tau = 0.3989422804014327


def gelu_slope(values):
    return 0.5 * (1.0 + lax.erf(values * half_root)) + values * jnp.exp(-0.5 * values * values) * inv_root_tau


def split_pairs(values):
    paired = values.reshape(values.shape[0], values.shape[1] // 2, 2)
    even_cols = paired[:, :, 0]
    odd_cols = paired[:, :, 1]
    return (even_cols + odd_cols) * half_root, (even_cols - odd_cols) * half_root


def pyramid(values, depth_count):
    coarse = values
    details = []
    sum_list = []
    for level_no in range(depth_count):
        coarse, detail = split_pairs(coarse)
        details.append(detail)
        sum_list.append(coarse)
    return details, sum_list, coarse


def stack_levels(part_list, out_type):
    filler = jnp.zeros((part_list[0].shape[0], 1), out_type)
    return jnp.concatenate([member.astype(out_type) for member in part_list] + [filler], axis=1)


def descend(adjoint, detail_cot, back_rows, depth_count, block_len):
    channels = adjoint.shape[0]
    for level_no in range(depth_count, 0, -1):
        width_now = block_len >> level_no
        first_col = block_len - 2 * width_now
        upward = detail_cot[:, first_col:first_col + width_now] + back_rows[:channels, first_col:first_col + width_now]
        even_cols = (adjoint + upward) * half_root
        odd_cols = (adjoint - upward) * half_root
        adjoint = jnp.stack([even_cols, odd_cols], axis=2).reshape(channels, 2 * width_now)
        if level_no > 1:
            lower_col = block_len - 4 * width_now
            adjoint = adjoint + back_rows[channels:, lower_col:lower_col + 2 * width_now]
    return adjoint


def block_backward(pressure_block, cot_block, fluid_block, top_adjoint, weight, block_len):
    depth_count = block_len.bit_length() - 1
    channels = pressure_block.shape[0]
    details, sum_list, coarse = pyramid(pressure_block.astype(jnp.float32), depth_count)
    stacked = jnp.concatenate([stack_levels(details, jnp.bfloat16), stack_levels(sum_list, jnp.bfloat16)], axis=0)
    mixed_rows = jnp.dot(weight, stacked, preferred_element_type=jnp.float32)
    start_cot = cot_block.astype(jnp.float32) * fluid_block.astype(jnp.float32)[None, :]
    cot_details, cot_sums, cot_top = pyramid(start_cot, depth_count)
    detail_cot = stack_levels(cot_details, jnp.float32)
    slopes = (detail_cot * gelu_slope(mixed_rows)).astype(jnp.bfloat16)
    back_rows = lax.dot_general(weight, slopes, (((0,), (0,)), ((), ())), preferred_element_type=jnp.float32)
    weight_part = lax.dot_general(slopes, stacked, (((1,), (1,)), ((), ())), preferred_element_type=jnp.float32)
    adjoint = top_adjoint + back_rows[channels:, block_len - 2:block_len - 1]
    return descend(adjoint, detail_cot, back_rows, depth_count, block_len), weight_part


def reference(pressure, cotangent, fluid_mask, weight):
    channels = pressure.shape[0]
    block_len = LEAF_DEV
    block_count = N_MORTON
    depth_count = block_len.bit_length() - 1
    coarse_count = block_count.bit_length() - 1
    pressure_blocks = pressure.reshape(channels, block_count, block_len).transpose(1, 0, 2)
    cot_blocks = cotangent.reshape(channels, block_count, block_len).transpose(1, 0, 2)
    fluid_blocks = fluid_mask.reshape(block_count, block_len)

    def block_tops(inputs):
        pressure_block, cot_block, fluid_block = inputs
        top_sum = pyramid(pressure_block.astype(jnp.float32), depth_count)[2]
        start_cot = cot_block.astype(jnp.float32) * fluid_block.astype(jnp.float32)[None, :]
        top_cot = pyramid(start_cot, depth_count)[2]
        return top_sum, top_cot

    top_sums, top_cots = lax.map(block_tops, (pressure_blocks, cot_blocks, fluid_blocks))
    sum_now = top_sums[:, :, 0].T
    cot_now = top_cots[:, :, 0].T
    weight_total = jnp.zeros((channels, 2 * channels), jnp.float32)
    detail_list = []
    back_list = []
    for bit_pos in range(coarse_count):
        sum_now, detail = split_pairs(sum_now)
        cot_now, cot_detail = split_pairs(cot_now)
        stacked = jnp.concatenate([detail.astype(jnp.bfloat16), sum_now.astype(jnp.bfloat16)], axis=0)
        mixed_rows = jnp.dot(weight, stacked, preferred_element_type=jnp.float32)
        slopes = (cot_detail * gelu_slope(mixed_rows)).astype(jnp.bfloat16)
        back_rows = lax.dot_general(weight, slopes, (((0,), (0,)), ((), ())), preferred_element_type=jnp.float32)
        weight_total = weight_total + lax.dot_general(slopes, stacked, (((1,), (1,)), ((), ())), preferred_element_type=jnp.float32)
        detail_list.append(cot_detail)
        back_list.append(back_rows)
    adjoint = cot_now + back_list[-1][channels:]
    for bit_pos in range(coarse_count - 1, -1, -1):
        upward = detail_list[bit_pos] + back_list[bit_pos][:channels]
        even_cols = (adjoint + upward) * half_root
        odd_cols = (adjoint - upward) * half_root
        adjoint = jnp.stack([even_cols, odd_cols], axis=2).reshape(channels, 2 * upward.shape[1])
        if bit_pos > 0:
            adjoint = adjoint + back_list[bit_pos - 1][channels:]
    top_adjoints = adjoint.T[:, :, None]

    def block_grads(inputs):
        pressure_block, cot_block, fluid_block, top_adjoint = inputs
        return block_backward(pressure_block, cot_block, fluid_block, top_adjoint, weight, block_len)

    pressure_grads, weight_parts = lax.map(block_grads, (pressure_blocks, cot_blocks, fluid_blocks, top_adjoints))
    grad_pressure = pressure_grads.transpose(1, 0, 2).reshape(channels, block_count * block_len)
    grad_weight = (weight_total + jnp.sum(weight_parts, axis=0)) * (LEAVES ** -0.5)
    return grad_pressure, grad_weight
```

```python
import functools

import jax
import jax.numpy as jnp
import numpy as np
from jax import lax
from jax.experimental import pallas as pl
from jax.experimental.pallas import tpu as pltpu
from jax.sharding import PartitionSpec as P

half_root = 0.7071067811865476
inv_root_tau = 0.3989422804014327
TILE = 256
CHUNKS = 2
LANES = 128
F32 = jnp.float32
BF16 = jnp.bfloat16
VMEM_LIMIT = 48 * 1024 * 1024


def gelu_slope(values):
    return (
        0.5 * (1.0 + lax.erf(values * half_root))
        + values * jnp.exp(-0.5 * values * values) * inv_root_tau
    )


def sign_tables(width, first_level):
    detail = np.zeros((width, width), np.float32)
    total = np.zeros((width, width), np.float32)
    scale = np.zeros((width,), np.float32)
    col = 0
    for level in range(1, width.bit_length()):
        span = 1 << level
        for first in range(0, width, span):
            middle = first + span // 2
            detail[first:middle, col] = 1.0
            detail[middle : first + span, col] = -1.0
            total[first : first + span, col] = 1.0
            scale[col] = half_root ** (first_level + level)
            col += 1
    return detail, total, scale


def fine_tables():
    detail, total, scale = sign_tables(TILE, 0)
    signs = np.concatenate([detail, total], axis=1)
    return signs, np.concatenate([scale, scale])[None, :]


def coarse_tables(tiles, blocks):
    tile_level = TILE.bit_length() - 1
    block_level = tile_level + tiles.bit_length() - 1
    detail = np.zeros((LANES, LANES), np.float32)
    total = np.zeros((LANES, LANES), np.float32)
    scale = np.zeros((LANES,), np.float32)
    for first, width, level in ((0, tiles, tile_level), (tiles, blocks, block_level)):
        part = slice(first, first + width)
        detail[part, part], total[part, part], scale[part] = sign_tables(width, level)
    return np.concatenate([detail, total], axis=1), np.concatenate([scale, scale])[None, :]


def dot(left, right):
    return jnp.dot(left, right, preferred_element_type=F32)


def dot_exact(left, right):
    return jnp.dot(left, right, preferred_element_type=F32, precision=lax.Precision.HIGHEST)


def dot_last(left, right):
    return lax.dot_general(left, right, (((1,), (1,)), ((), ())), preferred_element_type=F32)


def prep_kernel(ways, first_tile, ids_ref, press_ref, cot_ref, mask_ref, *outs):
    parts, tops_ref = outs[:ways], outs[ways]
    rows, width = press_ref.shape[0], parts[0].shape[1]
    own = ids_ref[0]
    tops = jnp.zeros(tops_ref.shape, F32)
    for step in range(ways):
        sub = lax.rem(own + ways - step, ways)
        lanes = pl.ds(pl.multiple_of(sub * width, width), width)
        kept = mask_ref[:, lanes].astype(F32).astype(BF16)
        parts[step][:rows, :] = press_ref[:, lanes]
        parts[step][rows:, :] = cot_ref[:, lanes] * kept
        leaf_tile = lax.broadcasted_iota(jnp.int32, (width, LANES), 0) // TILE
        lane = lax.broadcasted_iota(jnp.int32, (width, LANES), 1)
        place = jnp.where(lane - leaf_tile == first_tile + sub * (width // TILE), 1.0, 0.0)
        tops = tops + dot(parts[step][...], place.astype(BF16))
    tops_ref[...] = tops


def fine_kernel(ways, n_given, last, ids_ref, *refs):
    parts = refs[:ways]
    w_ref, wt_ref, signs_ref, back_ref, scale_ref = refs[ways : ways + 5]
    given = refs[ways + 5 : ways + 5 + n_given]
    outs = refs[ways + 5 + n_given : 2 * ways + 5 + n_given]
    grad_ref = refs[2 * ways + 5 + n_given]
    total_ref = refs[2 * ways + 6 + n_given] if last else grad_ref
    channels = w_ref.shape[0]
    rows = channels // ways
    if n_given:
        start = given[0][...]
        for one in given[1:]:
            start = start + one[...]
        total_ref[...] = start
    else:
        total_ref[...] = jnp.zeros(total_ref.shape, F32)

    def tile_step(tile):
        lanes = pl.ds(pl.multiple_of(tile * TILE, TILE), TILE)
        press = jnp.concatenate([part[:rows, lanes] for part in parts], axis=0)
        cot = jnp.concatenate([part[rows:, lanes] for part in parts], axis=0)
        scale = scale_ref[:, :TILE]
        detail = (dot(press, signs_ref[:, :TILE]) * scale).astype(BF16)
        total = (dot(press, signs_ref[:, TILE:]) * scale).astype(BF16)
        cot_detail = dot(cot, signs_ref[:, :TILE]) * scale
        mixed = dot(w_ref[:, :channels], detail) + dot(w_ref[:, channels:], total)
        slopes = (cot_detail * gelu_slope(mixed)).astype(BF16)
        up = (dot(wt_ref[:channels, :], slopes) * scale).astype(BF16)
        level = (dot(wt_ref[channels:, :], slopes) * scale).astype(BF16)
        spread = dot(up, back_ref[:TILE, :]) + dot(level, back_ref[TILE:, :])
        spread = spread.astype(BF16)
        for step in range(ways):
            outs[step][:, lanes] = spread[step * rows : (step + 1) * rows, :]
        total_ref[:channels, :] += dot_last(detail, slopes)
        total_ref[channels:, :] += dot_last(total, slopes)

    def pair(index, carry):
        tile_step(2 * index)
        tile_step(2 * index + 1)
        return carry

    lax.fori_loop(0, parts[0].shape[1] // TILE // 2, pair, 0)
    if last:
        own = ids_ref[0]
        for half in range(2):
            for step in range(ways):
                first = half * channels + step * rows
                group = half * channels + lax.rem(own + step, ways) * rows
                place = pl.ds(pl.multiple_of(group, rows), rows)
                for other in range(ways):
                    grad_ref[lax.rem(own + other, ways), place, :] = total_ref[
                        first : first + rows, other * rows : (other + 1) * rows
                    ].astype(BF16)


def coarse_kernel(ways, tiles, ids_ref, *refs):
    parts = refs[:ways]
    w_ref, wt_ref, signs_ref, back_ref, scale_ref, adjoint_ref, grad_ref = refs[ways:]
    channels = w_ref.shape[0]
    rows = channels // ways
    own, position = ids_ref[0], ids_ref[1]
    press = jnp.concatenate([part[:rows, :] for part in parts], axis=0)
    cot = jnp.concatenate([part[rows:, :] for part in parts], axis=0)
    scale = scale_ref[:, :LANES]
    detail = (dot_exact(press, signs_ref[:, :LANES]) * scale).astype(BF16)
    total = (dot_exact(press, signs_ref[:, LANES:]) * scale).astype(BF16)
    cot_detail = dot_exact(cot, signs_ref[:, :LANES]) * scale
    mixed = dot(w_ref[:, :channels], detail) + dot(w_ref[:, channels:], total)
    slopes = cot_detail * gelu_slope(mixed)
    up = dot(wt_ref[:rows, :], slopes.astype(BF16)) * scale
    level = dot(wt_ref[channels : channels + rows, :], slopes.astype(BF16)) * scale
    spread = dot_exact(up, back_ref[:LANES, :]) + dot_exact(level, back_ref[LANES:, :])
    lane = lax.broadcasted_iota(jnp.int32, spread.shape, 1)
    above = jnp.sum(jnp.where(lane == tiles + position, spread, 0.0), axis=1, keepdims=True)
    adjoint_ref[...] = spread + above
    lane = lax.broadcasted_iota(jnp.int32, slopes.shape, 1)
    counted = jnp.where(position == 0, LANES, tiles)
    counted = jnp.where(own == 0, counted, 0)
    slopes = jnp.where(lane < counted, slopes, 0.0).astype(BF16)
    grad_ref[:channels, :] = dot_last(detail, slopes)
    grad_ref[channels:, :] = dot_last(total, slopes)


def final_kernel(ways, first_tile, aliased, ids_ref, cot_ref, mask_ref, adjoint_ref, *refs):
    parts, out_ref = refs[:ways], refs[-1]
    width = parts[0].shape[1]
    own = ids_ref[0]
    lane = lax.broadcasted_iota(jnp.int32, adjoint_ref.shape, 1)
    for step in range(ways):
        sub = lax.rem(own + ways - step, ways)
        for tile in range(width // TILE):
            number = first_tile + sub * (width // TILE) + tile
            above = jnp.sum(
                jnp.where(lane == number, adjoint_ref[...], 0.0), axis=1, keepdims=True
            )
            lanes = pl.ds(pl.multiple_of(sub * width + tile * TILE, TILE), TILE)
            kept = mask_ref[:, lanes].astype(F32)
            out_ref[:, lanes] = (
                cot_ref[:, lanes].astype(F32) * kept
                + parts[step][:, tile * TILE : (tile + 1) * TILE].astype(F32)
                + above
            )


def vmem():
    return pl.BlockSpec(memory_space=pltpu.VMEM)


def smem():
    return pl.BlockSpec(memory_space=pltpu.SMEM)


def local(pressure, cotangent, fluid_mask, weight):
    rows, block_len = pressure.shape
    channels = weight.shape[0]
    ways = lax.axis_size("chan")
    blocks = lax.axis_size("morton")
    tiles = block_len // TILE
    leaf_total = block_len * blocks
    span = block_len // CHUNKS
    width = span // ways
    own = lax.axis_index("chan")
    ids = jnp.stack([own, lax.axis_index("morton")]).astype(jnp.int32)
    mask = fluid_mask.reshape(1, block_len)
    params = pltpu.CompilerParams(vmem_limit_bytes=VMEM_LIMIT)
    there = [[(i, (i - step) % ways) for i in range(ways)] for step in range(ways)]
    back = [[(i, (i + step) % ways) for i in range(ways)] for step in range(ways)]

    def chunk_spec(chunk, height):
        return pl.BlockSpec((height, span), lambda i: (0, chunk))

    def whole(shape):
        return pl.BlockSpec(shape, lambda i: (0, 0))

    arrived = []
    tops = None
    for chunk in range(CHUNKS):
        *cut, sums = pl.pallas_call(
            functools.partial(prep_kernel, ways, chunk * span // TILE),
            grid=(1,),
            in_specs=[smem()] + [chunk_spec(chunk, rows)] * 2 + [chunk_spec(chunk, 1)],
            out_specs=[whole((2 * rows, width))] * ways + [whole((2 * rows, LANES))],
            out_shape=[jax.ShapeDtypeStruct((2 * rows, width), BF16)] * ways
            + [jax.ShapeDtypeStruct((2 * rows, LANES), F32)],
            compiler_params=params,
            name="cut_leaves",
        )(ids, pressure, cotangent, mask)
        tops = sums if tops is None else tops + sums
        arrived.append(
            [cut[0]] + [lax.ppermute(cut[s], "chan", there[s]) for s in range(1, ways)]
        )

    block_tops = jnp.broadcast_to(jnp.sum(tops, axis=1)[None, :], (blocks, 2 * rows))
    all_tops = lax.all_to_all(block_tops, "morton", split_axis=0, concat_axis=0, tiled=True)
    filler = jnp.zeros((2 * rows, LANES - tiles - blocks), F32)
    tops = jnp.concatenate([tops[:, :tiles], all_tops.T, filler], axis=1)
    group_tops = [tops] + [lax.ppermute(tops, "chan", there[s]) for s in range(1, ways)]

    turn = own * rows
    mix = lax.dynamic_slice_in_dim(jnp.concatenate([weight, weight], 0), turn, channels, 0)
    mix = jnp.concatenate(
        [
            lax.dynamic_slice_in_dim(jnp.concatenate([half, half], 1), turn, channels, 1)
            for half in (mix[:, :channels], mix[:, channels:])
        ],
        axis=1,
    )
    mix_t = mix.T

    signs, scale = coarse_tables(tiles, blocks)
    adjoint, coarse_grad = pl.pallas_call(
        functools.partial(coarse_kernel, ways, tiles),
        in_specs=[smem()] + [vmem()] * (ways + 5),
        out_specs=[vmem()] * 2,
        out_shape=[
            jax.ShapeDtypeStruct((rows, LANES), F32),
            jax.ShapeDtypeStruct((2 * channels, channels), F32),
        ],
        compiler_params=params,
        name="coarse_levels",
    )(ids, *group_tops, mix, mix_t, jnp.asarray(signs), jnp.asarray(signs.T), jnp.asarray(scale))

    signs, scale = fine_tables()
    tables = (jnp.asarray(signs, BF16), jnp.asarray(signs.T, BF16), jnp.asarray(scale))
    grad = None
    returned = []
    for chunk in range(CHUNKS):
        last = chunk == CHUNKS - 1
        given = ([] if grad is None else [grad]) + ([coarse_grad] if last else [])
        grad_shape = (ways, 2 * channels, rows) if last else (2 * channels, channels)
        *spread, grad = pl.pallas_call(
            functools.partial(fine_kernel, ways, len(given), last),
            in_specs=[smem()] + [vmem()] * (ways + 5 + len(given)),
            out_specs=[vmem()] * (ways + 1),
            out_shape=[jax.ShapeDtypeStruct((rows, width), BF16)] * ways
            + [jax.ShapeDtypeStruct(grad_shape, BF16 if last else F32)],
            scratch_shapes=[pltpu.VMEM((2 * channels, channels), F32)] if last else [],
            compiler_params=params,
            name="fine_levels",
        )(ids, *arrived[chunk], mix, mix_t, *tables, *given)
        returned.append(
            [spread[0]] + [lax.ppermute(spread[s], "chan", back[s]) for s in range(1, ways)]
        )

    shares = lax.all_to_all(
        grad.reshape(ways * blocks, 2 * channels // blocks, rows),
        ("chan", "morton"),
        split_axis=0,
        concat_axis=0,
        tiled=True,
    )
    grad_weight = jnp.sum(shares.astype(F32), axis=0).T * leaf_total ** (-0.5)

    out = None
    for chunk in range(CHUNKS):
        carried = [] if out is None else [out]
        out = pl.pallas_call(
            functools.partial(final_kernel, ways, chunk * span // TILE, bool(carried)),
            grid=(1,),
            in_specs=[smem(), chunk_spec(chunk, rows), chunk_spec(chunk, 1), whole((rows, LANES))]
            + [whole((rows, width))] * ways
            + [pl.BlockSpec(memory_space=pl.ANY)] * len(carried),
            out_specs=chunk_spec(chunk, rows),
            out_shape=jax.ShapeDtypeStruct((rows, block_len), F32),
            input_output_aliases={4 + ways: 0} if carried else {},
            compiler_params=params,
            name="join_leaves",
        )(ids, cotangent, mask, adjoint, *returned[chunk], *carried)
    return (out, grad_weight)


def solution(mesh):
    placed = (P("chan", "morton"), P("chan", "morton"), P("morton"), P())
    return jax.shard_map(
        local,
        mesh=mesh,
        in_specs=placed,
        out_specs=(P("chan", "morton"), P("chan", "morton")),
        check_vma=False,
    )
```

```python
import functools

import jax
import jax.numpy as jnp
import numpy as np
from jax import lax
from jax.experimental import pallas as pl
from jax.experimental.pallas import tpu as pltpu
from jax.sharding import PartitionSpec as P

half_root = 0.7071067811865476
inv_root_tau = 0.3989422804014327
TILE = 256
SPANS = (10240, 6144)
BATCHES = (5, 6)
LANES = 128
F32 = jnp.float32
BF16 = jnp.bfloat16
VMEM_LIMIT = 60 * 1024 * 1024


def gelu_slope(values):
    return (
        0.5 * (1.0 + lax.erf(values * half_root))
        + values * jnp.exp(-0.5 * values * values) * inv_root_tau
    )


def sign_tables(width, first_level):
    detail = np.zeros((width, width), np.float32)
    total = np.zeros((width, width), np.float32)
    scale = np.zeros((width,), np.float32)
    col = 0
    for level in range(1, width.bit_length()):
        span = 1 << level
        for first in range(0, width, span):
            middle = first + span // 2
            detail[first:middle, col] = 1.0
            detail[middle : first + span, col] = -1.0
            total[first : first + span, col] = 1.0
            scale[col] = half_root ** (first_level + level)
            col += 1
    return detail, total, scale


def fine_tables():
    detail, total, scale = sign_tables(TILE, 0)
    signs = np.concatenate([detail, total], axis=1)
    return signs, np.concatenate([scale, scale])[None, :]


def coarse_tables(tiles, blocks):
    tile_level = TILE.bit_length() - 1
    block_level = tile_level + tiles.bit_length() - 1
    detail = np.zeros((LANES, LANES), np.float32)
    total = np.zeros((LANES, LANES), np.float32)
    scale = np.zeros((LANES,), np.float32)
    for first, width, level in ((0, tiles, tile_level), (tiles, blocks, block_level)):
        part = slice(first, first + width)
        detail[part, part], total[part, part], scale[part] = sign_tables(width, level)
    return np.concatenate([detail, total], axis=1), np.concatenate([scale, scale])[None, :]


def dot(left, right):
    return jnp.dot(left, right, preferred_element_type=F32)


def dot_exact(left, right):
    return jnp.dot(left, right, preferred_element_type=F32, precision=lax.Precision.HIGHEST)


def dot_last(left, right):
    return lax.dot_general(left, right, (((1,), (1,)), ((), ())), preferred_element_type=F32)


def started(src, dst, sem):
    copy = pltpu.make_async_copy(src, dst, sem)
    copy.start()
    return copy


def cut_kernel(ways, first, span, opening, ids_ref, press_ref, cot_ref, mask_ref, *refs):
    if opening:
        parts, sums_ref = refs[:ways], refs[ways]
        carry_buf, press_buf, cot_buf, mask_buf, in_sems, out_sems = refs[ways + 1 :]
    else:
        sums_ref, parts, spread_ref = refs[0], refs[1 : ways + 1], refs[ways + 1]
        press_buf, cot_buf, mask_buf, in_sems, out_sems = refs[ways + 2 :]
    rows, width = press_buf.shape[0], span // ways
    own = ids_ref[0]
    block_len = press_ref.shape[1]
    pieces = [(first + sub * width, width) for sub in range(ways)]
    if opening:
        pieces += [(start, min(width, block_len - start)) for start in range(span, block_len, width)]
    mask_copy = started(mask_ref.at[:, pl.ds(first, mask_buf.shape[1])], mask_buf, in_sems.at[0])
    fetched = []
    for number, (start, length) in enumerate(pieces):
        for which, (src, dst) in enumerate(((cot_ref, cot_buf), (press_ref, press_buf))):
            fetched.append(
                started(
                    src.at[:, pl.ds(start, length)],
                    dst.at[:, pl.ds(start - first, length)],
                    in_sems.at[1 + 2 * number + which],
                )
            )
    if not opening:
        spread_ref[...] = jnp.broadcast_to(sums_ref[:1, :], spread_ref.shape)
    half = LANES // 2
    sums = jnp.zeros((2 * rows, LANES), F32)
    lane = lax.broadcasted_iota(jnp.int32, (2 * rows, LANES), 1)
    ones = jnp.ones((TILE, LANES), BF16)
    mask_copy.wait()
    sent = []
    for number, (start, length) in enumerate(pieces):
        fetched[2 * number].wait()
        lanes = slice(start - first, start - first + length)
        kept = mask_buf[:, lanes].astype(F32).astype(BF16)
        cot_buf[:, lanes] = cot_buf[:, lanes] * kept
        fetched[2 * number + 1].wait()
        if number == ways - 1:
            for step in range(ways):
                sub = lax.rem(own + ways - step, ways)
                place = pl.ds(pl.multiple_of(sub * width, LANES), width)
                for which, src in enumerate((press_buf, cot_buf)):
                    sent.append(
                        started(
                            src.at[:, place],
                            parts[step].at[pl.ds(which * rows, rows), pl.ds(0, width)],
                            out_sems.at[2 * step + which],
                        )
                    )
        if opening:
            numbers = range((start - first) // TILE, (start - first + length) // TILE)
            stacked = []
            for tile in numbers:
                leaves = slice(tile * TILE, (tile + 1) * TILE)
                stacked += [press_buf[:, leaves], cot_buf[:, leaves]]
            found = dot(jnp.concatenate(stacked, axis=0), ones)
            for place, tile in enumerate(numbers):
                mine = found[place * 2 * rows : (place + 1) * 2 * rows, :]
                sums = jnp.where(lane % half == tile, mine, sums)
    if opening:
        high = sums.astype(BF16)
        rest = sums - high.astype(F32)
        middle = rest.astype(BF16)
        rest = rest - middle.astype(F32)
        upper = lane < half
        carry_buf[:, :LANES] = jnp.where(upper, high.astype(F32), middle.astype(F32)).astype(BF16)
        carry_buf[:, LANES:] = jnp.where(upper, rest, 0.0).astype(BF16)
        for step in range(ways):
            sent.append(
                started(
                    carry_buf,
                    parts[step].at[:, pl.ds(width, 2 * LANES)],
                    out_sems.at[2 * ways + step],
                )
            )
        block = jnp.sum(jnp.where(upper, sums, 0.0), axis=1, keepdims=True)
        sums_ref[...] = jnp.broadcast_to(block, sums.shape).T[:8, :]
    for copy in sent:
        copy.wait()


def fine_kernel(ways, n_given, batch, last, ids_ref, *refs):
    parts, refs = refs[:ways], refs[ways:]
    fixed, given, refs = refs[:5], refs[5 : 5 + n_given], refs[5 + n_given :]
    outs, grad_out, refs = refs[:ways], refs[ways], refs[ways + 1 :]
    part_buf, out_buf, total_ref, refs = refs[0], refs[1], refs[2], refs[3:]
    held, given_bufs, refs = refs[:5], refs[5 : 5 + n_given], refs[5 + n_given :]
    w_ref, wt_ref, signs_ref, back_ref, scale_ref = held
    grad_ref = refs[0] if last else total_ref
    in_sems, out_sems = refs[-2:]
    channels = w_ref.shape[0]
    rows = channels // ways
    width = out_buf.shape[2]
    steps = width // (batch * TILE)

    def run(index):
        return pl.ds(index * batch * TILE, batch * TILE)

    number = 5 + n_given
    fetched = [started(fixed[2], held[2], in_sems.at[2]), started(fixed[4], held[4], in_sems.at[4])]
    fetched_parts = []
    for index in range(steps):
        for step in range(ways):
            fetched_parts.append(
                started(
                    parts[step].at[:, run(index)], part_buf.at[step, :, run(index)], in_sems.at[number]
                )
            )
            number += 1
        if index == 0:
            fetched += [started(fixed[n], held[n], in_sems.at[n]) for n in (0, 1, 3)]
    fetched_given = [
        started(given[n], given_bufs[n], in_sems.at[5 + n]) for n in range(n_given)
    ]
    fetched[0].wait()
    fetched[1].wait()
    sent = []
    for index in range(steps):
        for copy in fetched_parts[index * ways : (index + 1) * ways]:
            copy.wait()
        here = [pl.ds((index * batch + tile) * TILE, TILE) for tile in range(batch)]

        def stacked(low):
            return jnp.concatenate(
                [part_buf[:, low : low + rows, lanes].reshape(channels, TILE) for lanes in here],
                axis=0,
            )

        def side_by_side(values):
            return jnp.concatenate(
                [values[tile * channels : (tile + 1) * channels] for tile in range(batch)], axis=1
            )

        def one_by_one(values):
            return jnp.concatenate(
                [
                    (values[:, tile * TILE : (tile + 1) * TILE] * scale).astype(BF16)
                    for tile in range(batch)
                ],
                axis=0,
            )

        scale = scale_ref[:, :TILE]
        press = stacked(0)
        detail = side_by_side((dot(press, signs_ref[:, :TILE]) * scale).astype(BF16))
        total = side_by_side((dot(press, signs_ref[:, TILE:]) * scale).astype(BF16))
        cot_detail = side_by_side(dot(stacked(rows), signs_ref[:, :TILE]) * scale)
        if index == 0:
            for copy in fetched[2:]:
                copy.wait()
        mixed = dot(w_ref[:, :channels], detail) + dot(w_ref[:, channels:], total)
        slopes = (cot_detail * gelu_slope(mixed)).astype(BF16)
        up = one_by_one(dot(wt_ref[:channels, :], slopes))
        level = one_by_one(dot(wt_ref[channels:, :], slopes))
        spread = (dot(up, back_ref[:TILE, :]) + dot(level, back_ref[TILE:, :])).astype(BF16)
        for tile, lanes in enumerate(here):
            out_buf[:, :, lanes] = spread[tile * channels : (tile + 1) * channels].reshape(
                ways, rows, TILE
            )
        for step in range(ways):
            sent.append(
                started(
                    out_buf.at[step, :, run(index)],
                    outs[step].at[:, run(index)],
                    out_sems.at[1 + index * ways + step],
                )
            )
        for half, values in enumerate((detail, total)):
            place = slice(half * channels, (half + 1) * channels)
            found = dot_last(values, slopes)
            if index:
                found = found + total_ref[place, :]
            else:
                for copy in fetched_given if half == 0 else ():
                    copy.wait()
                for one in given_bufs:
                    found = found + one[place, :]
            total_ref[place, :] = found
    if last:
        own = ids_ref[0]
        blocks = grad_ref.shape[0] // ways
        cols = 2 * channels // blocks
        for half in range(2):
            for step in range(ways):
                first = half * channels + step * rows
                group = half * channels + lax.rem(own + step, ways) * rows
                for other in range(ways):
                    share = total_ref[first : first + rows, other * rows : (other + 1) * rows]
                    share = share.reshape(rows // cols, 2, cols // 2, rows)
                    share = jnp.concatenate([share[:, 0], share[:, 1]], axis=2)
                    place = lax.rem(own + other, ways) * blocks + group // cols
                    grad_ref[pl.ds(place, rows // cols)] = share.astype(BF16)
    sent.append(started(grad_ref, grad_out, out_sems.at[0]))
    for copy in sent:
        copy.wait()


def coarse_kernel(ways, tiles, ids_ref, above_ref, *refs):
    parts = refs[:ways]
    w_ref, wt_ref, signs_ref, back_ref, scale_ref, adjoint_ref, grad_ref = refs[ways:]
    channels = w_ref.shape[0]
    rows = channels // ways
    own, position = ids_ref[0], ids_ref[1]
    blocks, half = above_ref.shape[0] // ways, LANES // 2
    tops = []
    for step, part in enumerate(parts):
        sums = part[...].astype(F32)
        inside = sums[:, :half] + sums[:, half:LANES] + sums[:, LANES : LANES + half]
        group = lax.rem(own + step, ways) * blocks
        outer = jnp.concatenate(
            [
                jnp.zeros((half, 2 * rows), F32),
                above_ref[pl.ds(pl.multiple_of(group, blocks), blocks), :],
                jnp.zeros((half - blocks, 2 * rows), F32),
            ],
            axis=0,
        )
        tops.append(jnp.concatenate([inside, outer.T[:, half:]], axis=1))
    press = jnp.concatenate([top[:rows, :] for top in tops], axis=0)
    cot = jnp.concatenate([top[rows:, :] for top in tops], axis=0)
    scale = scale_ref[:, :LANES]
    detail = (dot_exact(press, signs_ref[:, :LANES]) * scale).astype(BF16)
    total = (dot_exact(press, signs_ref[:, LANES:]) * scale).astype(BF16)
    cot_detail = dot_exact(cot, signs_ref[:, :LANES]) * scale
    mixed = dot(w_ref[:, :channels], detail) + dot(w_ref[:, channels:], total)
    slopes = cot_detail * gelu_slope(mixed)
    up = dot(wt_ref[:rows, :], slopes.astype(BF16)) * scale
    level = dot(wt_ref[channels : channels + rows, :], slopes.astype(BF16)) * scale
    spread = dot_exact(up, back_ref[:LANES, :]) + dot_exact(level, back_ref[LANES:, :])
    lane = lax.broadcasted_iota(jnp.int32, spread.shape, 1)
    above = jnp.sum(jnp.where(lane == tiles + position, spread, 0.0), axis=1, keepdims=True)
    adjoint_ref[...] = spread + above
    lane = lax.broadcasted_iota(jnp.int32, slopes.shape, 1)
    counted = jnp.where(position == 0, LANES, tiles)
    counted = jnp.where(own == 0, counted, 0)
    slopes = jnp.where(lane < counted, slopes, 0.0).astype(BF16)
    grad_ref[:channels, :] = dot_last(detail, slopes)
    grad_ref[channels:, :] = dot_last(total, slopes)


def shares_kernel(factor, shares_ref, out_ref):
    total = jnp.sum(shares_ref[...].astype(F32), axis=0)
    half = total.shape[1] // 2
    total = jnp.concatenate([total[:, :half], total[:, half:]], axis=0)
    out_ref[...] = total * factor


def final_kernel(ways, first, ids_ref, cot_ref, mask_ref, adjoint_ref, *refs):
    parts = refs[:ways]
    out_ref, cot_buf, mask_buf, part_buf, out_buf, sems = refs[-6:]
    width = parts[0].shape[1]
    span = ways * width
    own = ids_ref[0]
    mask_copy = started(mask_ref.at[:, pl.ds(first, span)], mask_buf, sems.at[0])
    places, fetched = [], []
    for step in range(ways):
        start = pl.multiple_of(lax.rem(own + ways - step, ways) * width, TILE)
        places.append(start)
        fetched.append(
            started(
                cot_ref.at[:, pl.ds(first + start, width)],
                cot_buf.at[:, pl.ds(start, width)],
                sems.at[1 + step],
            )
        )
        fetched.append(started(parts[step], part_buf.at[step], sems.at[1 + ways + step]))
    mask_copy.wait()
    lane = lax.broadcasted_iota(jnp.int32, adjoint_ref.shape, 1)
    sent = []
    for step, start in enumerate(places):
        fetched[2 * step].wait()
        fetched[2 * step + 1].wait()
        for tile in range(width // TILE):
            number = (first + start) // TILE + tile
            above = jnp.sum(
                jnp.where(lane == number, adjoint_ref[...], 0.0), axis=1, keepdims=True
            )
            lanes = pl.ds(pl.multiple_of(start + tile * TILE, TILE), TILE)
            kept = mask_buf[:, lanes].astype(F32)
            out_buf[:, lanes] = (
                cot_buf[:, lanes].astype(F32) * kept
                + part_buf[step, :, tile * TILE : (tile + 1) * TILE].astype(F32)
                + above
            )
        sent.append(
            started(
                out_buf.at[:, pl.ds(start, width)],
                out_ref.at[:, pl.ds(first + start, width)],
                sems.at[1 + 2 * ways + step],
            )
        )
    for copy in sent:
        copy.wait()


def vmem():
    return pl.BlockSpec(memory_space=pltpu.VMEM)


def smem():
    return pl.BlockSpec(memory_space=pltpu.SMEM)


def local(pressure, cotangent, fluid_mask, weight):
    rows, block_len = pressure.shape
    channels = weight.shape[0]
    ways = lax.axis_size("chan")
    blocks = lax.axis_size("morton")
    tiles = block_len // TILE
    leaf_total = block_len * blocks
    own = lax.axis_index("chan")
    ids = jnp.stack([own, lax.axis_index("morton")]).astype(jnp.int32)
    mask = fluid_mask.reshape(1, block_len)
    params = pltpu.CompilerParams(vmem_limit_bytes=VMEM_LIMIT)
    there = [[(i, (i - step) % ways) for i in range(ways)] for step in range(ways)]
    back = [[(i, (i + step) % ways) for i in range(ways)] for step in range(ways)]
    starts = [sum(SPANS[:number]) for number in range(len(SPANS))]
    hbm = pl.BlockSpec(memory_space=pltpu.HBM)

    arrived = []
    carried = []
    for number, (first, span) in enumerate(zip(starts, SPANS)):
        opening = number == 0
        width = span // ways + (2 * LANES if opening else 0)
        held = block_len if opening else span
        *cut, sums = pl.pallas_call(
            functools.partial(cut_kernel, ways, first, span, opening),
            in_specs=[smem()] + [hbm] * 3 + [vmem()] * len(carried),
            out_specs=[hbm] * ways + [vmem()],
            out_shape=[jax.ShapeDtypeStruct((2 * rows, width), BF16)] * ways
            + [jax.ShapeDtypeStruct((8 if opening else ways * blocks, LANES), F32)],
            scratch_shapes=([pltpu.VMEM((2 * rows, 2 * LANES), BF16)] if opening else [])
            + [
                pltpu.VMEM((rows, held), BF16),
                pltpu.VMEM((rows, held), BF16),
                pltpu.VMEM((1, held), jnp.int32),
                pltpu.SemaphoreType.DMA((1 + 2 * (ways + -(-block_len // span) * ways),)),
                pltpu.SemaphoreType.DMA((3 * ways,)),
            ],
            compiler_params=params,
            name="cut_leaves",
        )(ids, pressure, cotangent, mask, *carried)
        if opening:
            carried = [sums]
        arrived.append(
            [cut[0]] + [lax.ppermute(cut[s], "chan", there[s]) for s in range(1, ways)]
        )
    lanes = SPANS[0] // ways
    all_tops = lax.all_to_all(sums, ("chan", "morton"), split_axis=0, concat_axis=0, tiled=True)

    turn = own * rows
    mix = lax.dynamic_slice_in_dim(jnp.concatenate([weight, weight], 0), turn, channels, 0)
    mix = jnp.concatenate(
        [
            lax.dynamic_slice_in_dim(jnp.concatenate([half, half], 1), turn, channels, 1)
            for half in (mix[:, :channels], mix[:, channels:])
        ],
        axis=1,
    )
    mix_t = mix.T

    signs, scale = coarse_tables(tiles, blocks)

    def whole(*shape):
        return pl.BlockSpec(shape, lambda i: (0,) * len(shape))

    adjoint, coarse_grad = pl.pallas_call(
        functools.partial(coarse_kernel, ways, tiles),
        grid=(1,),
        in_specs=[smem(), whole(ways * blocks, LANES)]
        + [pl.BlockSpec((2 * rows, 2 * LANES), lambda i: (0, lanes // (2 * LANES)))] * ways
        + [
            whole(channels, 2 * channels),
            whole(2 * channels, channels),
            whole(LANES, 2 * LANES),
            whole(2 * LANES, LANES),
            whole(1, 2 * LANES),
        ],
        out_specs=[whole(rows, LANES), whole(2 * channels, channels)],
        out_shape=[
            jax.ShapeDtypeStruct((rows, LANES), F32),
            jax.ShapeDtypeStruct((2 * channels, channels), F32),
        ],
        compiler_params=params,
        name="coarse_levels",
    )(
        ids,
        all_tops,
        *arrived[0],
        mix,
        mix_t,
        jnp.asarray(signs),
        jnp.asarray(signs.T),
        jnp.asarray(scale),
    )

    signs, scale = fine_tables()
    tables = (jnp.asarray(signs, BF16), jnp.asarray(signs.T, BF16), jnp.asarray(scale))
    grad = None
    returned = []
    arrived[0][0], all_tops = lax.optimization_barrier((arrived[0][0], all_tops))
    for number, (span, batch) in enumerate(zip(SPANS, BATCHES)):
        last = number == len(SPANS) - 1
        given = ([] if grad is None else [grad]) + ([coarse_grad] if last else [])
        share = 2 * channels * rows // blocks // LANES
        grad_shape = (ways * blocks, share, LANES) if last else (2 * channels, channels)
        *spread, grad = pl.pallas_call(
            functools.partial(fine_kernel, ways, len(given), batch, last),
            in_specs=[smem()] + [hbm] * (ways + 5 + len(given)),
            out_specs=[hbm] * (ways + 1),
            out_shape=[jax.ShapeDtypeStruct((rows, span // ways), BF16)] * ways
            + [jax.ShapeDtypeStruct(grad_shape, BF16 if last else F32)],
            scratch_shapes=[
                pltpu.VMEM((ways, 2 * rows, span // ways), BF16),
                pltpu.VMEM((ways, rows, span // ways), BF16),
                pltpu.VMEM((2 * channels, channels), F32),
            ]
            + [pltpu.VMEM(one.shape, one.dtype) for one in (mix, mix_t, *tables, *given)]
            + ([pltpu.VMEM(grad_shape, BF16)] if last else [])
            + [
                pltpu.SemaphoreType.DMA((5 + len(given) + ways * (span // ways // TILE),)),
                pltpu.SemaphoreType.DMA((1 + ways * (span // ways // TILE),)),
            ],
            compiler_params=params,
            name="fine_levels",
        )(ids, *arrived[number], mix, mix_t, *tables, *given)
        returned.append(
            [spread[0]] + [lax.ppermute(spread[s], "chan", back[s]) for s in range(1, ways)]
        )

    shares = lax.all_to_all(grad, ("chan", "morton"), split_axis=0, concat_axis=0, tiled=True)
    grad_weight = pl.pallas_call(
        functools.partial(shares_kernel, leaf_total ** (-0.5)),
        in_specs=[vmem()],
        out_specs=vmem(),
        out_shape=jax.ShapeDtypeStruct((2 * channels // blocks, rows), F32),
        compiler_params=params,
        name="sum_shares",
    )(shares).T

    out = None
    for number, (first, span) in enumerate(zip(starts, SPANS)):
        carried = [] if out is None else [out]
        out = pl.pallas_call(
            functools.partial(final_kernel, ways, first),
            in_specs=[smem(), hbm, hbm, vmem()] + [hbm] * (ways + len(carried)),
            out_specs=hbm,
            out_shape=jax.ShapeDtypeStruct((rows, block_len), F32),
            scratch_shapes=[
                pltpu.VMEM((rows, span), BF16),
                pltpu.VMEM((1, span), jnp.int32),
                pltpu.VMEM((ways, rows, span // ways), BF16),
                pltpu.VMEM((rows, span), F32),
                pltpu.SemaphoreType.DMA((1 + 3 * ways,)),
            ],
            input_output_aliases={4 + ways: 0} if carried else {},
            compiler_params=params,
            name="join_leaves",
        )(ids, cotangent, mask, adjoint, *returned[number], *carried)
    return (out, grad_weight)


def solution(mesh):
    placed = (P("chan", "morton"), P("chan", "morton"), P("morton"), P())
    return jax.shard_map(
        local,
        mesh=mesh,
        in_specs=placed,
        out_specs=(P("chan", "morton"), P("chan", "morton")),
        check_vma=False,
    )
```

```python
import functools

import jax
import jax.numpy as jnp
import numpy as np
from jax import lax
from jax.experimental import pallas as pl
from jax.experimental.pallas import tpu as pltpu
from jax.sharding import PartitionSpec as P

half_root = 0.7071067811865476
inv_root_tau = 0.3989422804014327
TILE = 256
SPANS = (12288, 4096)
BATCHES = ((6, 6), (4,))
LANES = 128
F32 = jnp.float32
BF16 = jnp.bfloat16
MIB = 1024 * 1024
HOLD = 1
HOLD_BACK = False
FINE_MIB = 40
JOIN_MIB = 16
CUT_MIB = 16


def gelu_slope(values):
    return (
        0.5 * (1.0 + lax.erf(values * half_root))
        + values * jnp.exp(-0.5 * values * values) * inv_root_tau
    )


def sign_tables(width, first_level):
    detail = np.zeros((width, width), np.float32)
    total = np.zeros((width, width), np.float32)
    scale = np.zeros((width,), np.float32)
    col = 0
    for level in range(1, width.bit_length()):
        span = 1 << level
        for first in range(0, width, span):
            middle = first + span // 2
            detail[first:middle, col] = 1.0
            detail[middle : first + span, col] = -1.0
            total[first : first + span, col] = 1.0
            scale[col] = half_root ** (first_level + level)
            col += 1
    return detail, total, scale


def fine_tables():
    detail, total, scale = sign_tables(TILE, 0)
    signs = np.concatenate([detail, total], axis=1)
    return signs, np.concatenate([scale, scale])[None, :]


def coarse_tables(tiles, blocks):
    tile_level = TILE.bit_length() - 1
    block_level = tile_level + tiles.bit_length() - 1
    detail = np.zeros((LANES, LANES), np.float32)
    total = np.zeros((LANES, LANES), np.float32)
    scale = np.zeros((LANES,), np.float32)
    for first, width, level in ((0, tiles, tile_level), (tiles, blocks, block_level)):
        part = slice(first, first + width)
        detail[part, part], total[part, part], scale[part] = sign_tables(width, level)
    signs = np.concatenate([detail, total], axis=1)
    spread = np.zeros((2 * LANES, 2 * LANES), np.float32)
    for copy in range(2):
        spread[copy * tiles : (copy + 1) * tiles] = signs[:tiles]
        first = LANES + copy * blocks
        spread[first : first + blocks] = signs[tiles : tiles + blocks]
    return spread, signs.T, scale[None, :]


def dot(left, right):
    return jnp.dot(left, right, preferred_element_type=F32)


def dot_last(left, right):
    return lax.dot_general(left, right, (((1,), (1,)), ((), ())), preferred_element_type=F32)


def started(src, dst, sem):
    copy = pltpu.make_async_copy(src, dst, sem)
    copy.start()
    return copy


def in_two(values):
    high = values.astype(BF16).astype(F32)
    return high, values - high


def sums_kernel(ways, press_ref, cot_ref, mask_ref, carry_ref, spread_ref, *refs):
    press_buf, cot_buf, mask_buf, carry_buf, spread_buf, in_sems, out_sems = refs
    rows, block_len = press_buf.shape
    width = block_len // ways
    mask_copy = started(mask_ref, mask_buf, in_sems.at[0])
    runs = [pl.ds(sub * width, width) for sub in range(ways)]
    fetched = []
    for sub, run in enumerate(runs):
        fetched.append(started(cot_ref.at[:, run], cot_buf.at[:, run], in_sems.at[1 + 2 * sub]))
        fetched.append(started(press_ref.at[:, run], press_buf.at[:, run], in_sems.at[2 + 2 * sub]))
    half = LANES // 2
    sums = jnp.zeros((2 * rows, LANES), F32)
    lane = lax.broadcasted_iota(jnp.int32, (2 * rows, LANES), 1)
    ones = jnp.ones((TILE, LANES), BF16)
    mask_copy.wait()
    for sub in range(ways):
        fetched[2 * sub].wait()
        fetched[2 * sub + 1].wait()
        numbers = range(sub * width // TILE, (sub + 1) * width // TILE)
        stacked = []
        for tile in numbers:
            leaves = slice(tile * TILE, (tile + 1) * TILE)
            kept = mask_buf[:, leaves].astype(F32).astype(BF16)
            stacked += [press_buf[:, leaves], cot_buf[:, leaves] * kept]
        found = dot(jnp.concatenate(stacked, axis=0), ones)
        for place, tile in enumerate(numbers):
            mine = found[place * 2 * rows : (place + 1) * 2 * rows, :]
            sums = jnp.where(lane % half == tile, mine, sums)
    upper = lane < half
    block = jnp.sum(jnp.where(upper, sums, 0.0), axis=1, keepdims=True)
    row = jnp.broadcast_to(block, sums.shape).T[:1, :]
    spread_buf[...] = jnp.broadcast_to(row, spread_buf.shape)
    sent = [started(spread_buf, spread_ref, out_sems.at[0])]
    high, rest = in_two(sums)
    carry_buf[...] = jnp.where(upper, high, rest).astype(BF16)
    sent.append(started(carry_buf, carry_ref, out_sems.at[1]))
    for copy in sent:
        copy.wait()


def cut_kernel(ways, first, span, closing, press_ref, cot_ref, mask_ref, *refs):
    if closing:
        carry_ref, above_ref, joined_ref, refs = refs[0], refs[1], refs[2], refs[3:]
    else:
        parts, refs = refs[:ways], refs[ways:]
    press_buf, cot_buf, mask_buf, in_sems, out_sems = refs[-5:]
    rows, width = press_buf.shape[0], span // ways
    own = lax.axis_index("chan")
    mask_copy = started(mask_ref.at[:, pl.ds(first, span)], mask_buf, in_sems.at[0])
    fetched, places = [], []
    for step in range(ways):
        start = pl.multiple_of(lax.rem(own + ways - step, ways) * width, LANES)
        run, place = pl.ds(first + start, width), pl.ds(start, width)
        places.append(place)
        fetched.append(started(cot_ref.at[:, run], cot_buf.at[:, place], in_sems.at[1 + 2 * step]))
        fetched.append(
            started(press_ref.at[:, run], press_buf.at[:, place], in_sems.at[2 + 2 * step])
        )
    sent = []
    if closing:
        carry_buf, above_buf = refs[:2]
        parts = [joined_ref.at[lax.rem(own + ways - step, ways)] for step in range(ways)]
        carried = [
            started(above_ref, above_buf, in_sems.at[1 + 2 * ways]),
            started(carry_ref, carry_buf.at[:, pl.ds(0, LANES)], in_sems.at[2 + 2 * ways]),
        ]
        carried[0].wait()
        outer = list(in_two(above_buf[...]))
        outer.append(jnp.zeros((LANES - 2 * above_buf.shape[0], LANES), F32))
        carry_buf[:, LANES:] = jnp.concatenate(outer, axis=0).T.astype(BF16)
        carried[1].wait()
        for step in range(ways):
            place = parts[step].at[:, pl.ds(width, 2 * LANES)]
            sent.append(started(carry_buf, place, out_sems.at[2 * ways + step]))
    mask_copy.wait()
    for step, place in enumerate(places):
        fetched[2 * step].wait()
        cot_buf[:, place] = cot_buf[:, place] * mask_buf[:, place].astype(F32).astype(BF16)
        dst = parts[step].at[pl.ds(rows, rows), pl.ds(0, width)]
        sent.append(started(cot_buf.at[:, place], dst, out_sems.at[2 * step]))
        fetched[2 * step + 1].wait()
        dst = parts[step].at[pl.ds(0, rows), pl.ds(0, width)]
        sent.append(started(press_buf.at[:, place], dst, out_sems.at[2 * step + 1]))
    for copy in sent:
        copy.wait()


def fine_kernel(ways, batches, tiles, last, *refs):
    n_given = 6 if last else 5
    own, position = lax.axis_index("chan"), lax.axis_index("morton")
    if last:
        parts = [refs[0].at[lax.rem(own + step, ways)] for step in range(ways)]
        refs = refs[1:]
    else:
        parts, refs = refs[:ways], refs[ways:]
    given, refs = refs[:n_given], refs[n_given:]
    if last:
        grad_in, refs = refs[0], refs[1:]
    outs, grad_out, refs = refs[:ways], refs[ways], refs[ways + 1 :]
    if last:
        adjoint_ref, refs = refs[0], refs[1:]
    part_buf, out_buf, total_ref, refs = refs[0], refs[1], refs[2], refs[3:]
    held, refs = refs[:n_given], refs[n_given:]
    w_ref, wt_ref, signs_ref, back_ref, scale_ref = held[:5]
    if last:
        coarse_ref = held[5]
        adjoint_buf, grad_ref, refs = refs[0], refs[1], refs[2:]
    else:
        grad_ref = total_ref
    in_sems, out_sems = refs[-2:]
    channels = w_ref.shape[0]
    rows = channels // ways
    width = out_buf.shape[2]
    starts = [sum(batches[:index]) * TILE for index in range(len(batches))]
    runs = [pl.ds(start, batch * TILE) for start, batch in zip(starts, batches)]

    fetched = [None] * n_given
    for n in (2, 4):
        fetched[n] = started(given[n], held[n], in_sems.at[n])
    number = n_given
    fetched_parts = []
    for index, run in enumerate(runs):
        if last and index == len(runs) - 1:
            run = pl.ds(starts[index], width + 2 * LANES - starts[index])
        for step in range(ways):
            fetched_parts.append(
                started(parts[step].at[:, run], part_buf.at[step, :, run], in_sems.at[number])
            )
            number += 1
        if index == 0:
            for n in (0, 1, 3):
                fetched[n] = started(given[n], held[n], in_sems.at[n])
    if last:
        fetched[5] = started(given[5], held[5], in_sems.at[5])
        fetched_grad = started(grad_in, total_ref, in_sems.at[number])
    fetched[2].wait()
    fetched[4].wait()
    scale = scale_ref[:1, :]
    sent = []
    for index, run in enumerate(runs):
        batch = batches[index]
        closing = last and index == len(runs) - 1
        for copy in fetched_parts[index * ways : (index + 1) * ways]:
            copy.wait()
        here = [pl.ds(starts[index] + tile * TILE, TILE) for tile in range(batch)]

        def stacked(low):
            return jnp.concatenate(
                [part_buf[:, low : low + rows, lanes].reshape(channels, TILE) for lanes in here],
                axis=0,
            )

        def side_by_side(values):
            return [values[tile * channels : (tile + 1) * channels] for tile in range(batch)]

        def one_by_one(values):
            return jnp.concatenate(
                [
                    (values[:, tile * TILE : (tile + 1) * TILE] * scale).astype(BF16)
                    for tile in range(batch)
                ],
                axis=0,
            )

        press = stacked(0)
        detail = side_by_side((dot(press, signs_ref[:, :TILE]) * scale).astype(BF16))
        total = side_by_side((dot(press, signs_ref[:, TILE:]) * scale).astype(BF16))
        cot_detail = side_by_side(dot(stacked(rows), signs_ref[:, :TILE]) * scale)
        if closing:
            fetched[5].wait()
            tops = [part_buf[step, :, width:] for step in range(ways)]
            tops = [top[:rows] for top in tops] + [top[rows:] for top in tops]
            found = dot(jnp.concatenate(tops, axis=0), coarse_ref[: 2 * LANES, :])
            coarse_scale = scale_ref[1:2, :LANES]
            detail.append((found[:channels, :LANES] * coarse_scale).astype(BF16))
            total.append((found[:channels, LANES:] * coarse_scale).astype(BF16))
            cot_detail.append(found[channels:, :LANES] * coarse_scale)
        if index == 0:
            for n in (0, 1, 3):
                fetched[n].wait()
        detail, total = jnp.concatenate(detail, axis=1), jnp.concatenate(total, axis=1)
        mixed = dot(w_ref[:, :channels], detail) + dot(w_ref[:, channels:], total)
        slopes = (jnp.concatenate(cot_detail, axis=1) * gelu_slope(mixed)).astype(BF16)
        up = dot(wt_ref[:channels, :], slopes)
        level = dot(wt_ref[channels:, :], slopes)
        spread = dot(one_by_one(up), back_ref[:TILE, :])
        spread = (spread + dot(one_by_one(level), back_ref[TILE:, :])).astype(BF16)
        for tile, lanes in enumerate(here):
            out_buf[:, :, lanes] = spread[tile * channels : (tile + 1) * channels].reshape(
                ways, rows, TILE
            )
        for step in range(ways):
            sent.append(
                started(
                    out_buf.at[step, :, run],
                    outs[step].at[:, run],
                    out_sems.at[2 + index * ways + step],
                )
            )
        if closing:
            coarse = batch * TILE
            nodes = jnp.concatenate(
                [
                    (values[:rows, coarse:] * coarse_scale).astype(BF16)
                    for values in (up, level)
                ],
                axis=1,
            )
            back = jnp.concatenate(
                [coarse_ref[2 * LANES : 3 * LANES, :], coarse_ref[3 * LANES :, :]], axis=0
            )[:, :LANES]
            adjoint = dot(nodes, back)
            lane = lax.broadcasted_iota(jnp.int32, adjoint.shape, 1)
            above = jnp.where(lane == tiles + position, adjoint, 0.0)
            adjoint_buf[...] = adjoint + jnp.sum(above, axis=1, keepdims=True)
            sent.append(started(adjoint_buf, adjoint_ref, out_sems.at[1]))
            counted = jnp.where(position == 0, LANES, tiles)
            counted = jnp.where(own == 0, counted, 0)
            lane = lax.broadcasted_iota(jnp.int32, (channels, LANES), 1)
            shown = jnp.where(lane < counted, slopes[:, coarse:].astype(F32), 0.0).astype(BF16)
            slopes = jnp.concatenate([slopes[:, :coarse], shown], axis=1)
            fetched_grad.wait()
        for half, values in enumerate((detail, total)):
            place = slice(half * channels, (half + 1) * channels)
            found = dot_last(values, slopes)
            if index or last:
                found = found + total_ref[place, :]
            total_ref[place, :] = found
    if last:
        blocks = grad_ref.shape[0] // ways
        cols = 2 * channels // blocks
        for half in range(2):
            for step in range(ways):
                first = half * channels + step * rows
                group = half * channels + lax.rem(own + step, ways) * rows
                for other in range(ways):
                    share = total_ref[first : first + rows, other * rows : (other + 1) * rows]
                    share = share.reshape(rows // cols, 2, cols // 2, rows)
                    share = jnp.concatenate([share[:, 0], share[:, 1]], axis=2)
                    place = lax.rem(own + other, ways) * blocks + group // cols
                    grad_ref[pl.ds(place, rows // cols)] = share.astype(BF16)
    sent.append(started(grad_ref, grad_out, out_sems.at[0]))
    for copy in sent:
        copy.wait()


def shares_kernel(factor, shares_ref, out_ref):
    total = jnp.sum(shares_ref[...].astype(F32), axis=0)
    half = total.shape[1] // 2
    out_ref[...] = jnp.concatenate([total[:, :half], total[:, half:]], axis=0) * factor


def join_kernel(ways, first, cot_ref, mask_ref, adjoint_ref, *refs):
    parts = refs[:ways]
    out_ref, adjoint_buf, cot_buf, mask_buf, part_buf, out_buf, sems = refs[-7:]
    width = parts[0].shape[1]
    span = ways * width
    own = lax.axis_index("chan")
    opening = [
        started(mask_ref.at[:, pl.ds(first, span)], mask_buf, sems.at[0]),
        started(adjoint_ref, adjoint_buf, sems.at[1]),
    ]
    places, fetched = [], []
    for step in range(ways):
        start = pl.multiple_of(lax.rem(own + ways - step, ways) * width, TILE)
        places.append(start)
        fetched.append(
            started(
                cot_ref.at[:, pl.ds(first + start, width)],
                cot_buf.at[:, pl.ds(start, width)],
                sems.at[2 + step],
            )
        )
        fetched.append(started(parts[step], part_buf.at[step], sems.at[2 + ways + step]))
    for copy in opening:
        copy.wait()
    lane = lax.broadcasted_iota(jnp.int32, adjoint_buf.shape, 1)
    sent = []
    for step, start in enumerate(places):
        fetched[2 * step].wait()
        fetched[2 * step + 1].wait()
        for tile in range(width // TILE):
            number = (first + start) // TILE + tile
            above = jnp.sum(
                jnp.where(lane == number, adjoint_buf[...], 0.0), axis=1, keepdims=True
            )
            lanes = pl.ds(pl.multiple_of(start + tile * TILE, TILE), TILE)
            kept = mask_buf[:, lanes].astype(F32)
            out_buf[:, lanes] = (
                cot_buf[:, lanes].astype(F32) * kept
                + part_buf[step, :, tile * TILE : (tile + 1) * TILE].astype(F32)
                + above
            )
        sent.append(
            started(
                out_buf.at[:, pl.ds(start, width)],
                out_ref.at[:, pl.ds(first + start, width)],
                sems.at[2 + 2 * ways + step],
            )
        )
    for copy in sent:
        copy.wait()


def in_hbm(*arrays):
    return [pltpu.with_memory_space_constraint(array, pltpu.HBM) for array in arrays]


def held_in(parts):
    return in_hbm(parts[0]) + parts[1:]


def scoped(mib):
    return pltpu.CompilerParams(vmem_limit_bytes=mib * MIB)


def local(pressure, cotangent, fluid_mask, weight):
    rows, block_len = pressure.shape
    channels = weight.shape[0]
    ways = lax.axis_size("chan")
    blocks = lax.axis_size("morton")
    tiles = block_len // TILE
    leaf_total = block_len * blocks
    own = lax.axis_index("chan")
    mask = fluid_mask.reshape(1, block_len)
    there = [[(i, (i - step) % ways) for i in range(ways)] for step in range(ways)]
    back = [[(i, (i + step) % ways) for i in range(ways)] for step in range(ways)]
    starts = [sum(SPANS[:number]) for number in range(len(SPANS))]
    hbm = pl.BlockSpec(memory_space=pltpu.HBM)
    either = pl.BlockSpec(memory_space=pl.ANY)

    def cut(number, *carried):
        first, span = starts[number], SPANS[number]
        width = span // ways + (2 * LANES if carried else 0)
        parts = pl.pallas_call(
            functools.partial(cut_kernel, ways, first, span, bool(carried)),
            in_specs=[hbm] * (3 + len(carried)),
            out_specs=[hbm] * (1 if carried else ways),
            out_shape=[pltpu.HBM((ways, 2 * rows, width), BF16)]
            if carried
            else [pltpu.HBM((2 * rows, width), BF16)] * ways,
            scratch_shapes=[
                pltpu.VMEM((2 * rows, 2 * LANES), BF16),
                pltpu.VMEM((blocks, LANES), F32),
            ][: len(carried)]
            + [
                pltpu.VMEM((rows, span), BF16),
                pltpu.VMEM((rows, span), BF16),
                pltpu.VMEM((1, span), jnp.int32),
                pltpu.SemaphoreType.DMA((3 + 2 * ways,)),
                pltpu.SemaphoreType.DMA((3 * ways,)),
            ],
            compiler_params=scoped(CUT_MIB),
            name="cut_leaves",
        )(*in_hbm(pressure, cotangent, mask, *carried))
        if carried:
            return [lax.all_to_all(parts[0], "chan", split_axis=0, concat_axis=0, tiled=True)]
        return [parts[0]] + [lax.ppermute(parts[s], "chan", there[s]) for s in range(1, ways)]

    arrived = [cut(0)]
    carry, block_sums = pl.pallas_call(
        functools.partial(sums_kernel, ways),
        in_specs=[hbm] * 3,
        out_specs=[hbm] * 2,
        out_shape=[pltpu.HBM((2 * rows, LANES), BF16), pltpu.HBM((blocks, LANES), F32)],
        scratch_shapes=[
            pltpu.VMEM((rows, block_len), BF16),
            pltpu.VMEM((rows, block_len), BF16),
            pltpu.VMEM((1, block_len), jnp.int32),
            pltpu.VMEM((2 * rows, LANES), BF16),
            pltpu.VMEM((blocks, LANES), F32),
            pltpu.SemaphoreType.DMA((1 + 2 * ways,)),
            pltpu.SemaphoreType.DMA((2,)),
        ],
        compiler_params=scoped(CUT_MIB),
        name="sum_tiles",
    )(*in_hbm(pressure, cotangent, mask))
    block_sums = lax.all_to_all(block_sums, "morton", split_axis=0, concat_axis=0, tiled=True)
    arrived.append(cut(1, carry, block_sums))

    turn = own * rows
    mix = lax.dynamic_slice_in_dim(jnp.concatenate([weight, weight], 0), turn, channels, 0)
    mix = jnp.concatenate(
        [
            lax.dynamic_slice_in_dim(jnp.concatenate([half, half], 1), turn, channels, 1)
            for half in (mix[:, :channels], mix[:, channels:])
        ],
        axis=1,
    )
    signs, fine_scale = fine_tables()
    coarse, coarse_back, coarse_scale = coarse_tables(tiles, blocks)
    scale = np.zeros((8, TILE), np.float32)
    scale[0] = fine_scale[0, :TILE]
    scale[1, :LANES] = coarse_scale[0]
    coarse = np.concatenate([coarse, np.pad(coarse_back, ((0, 0), (0, LANES)))], axis=0)
    tables = [
        mix,
        mix.T,
        jnp.asarray(signs, BF16),
        jnp.asarray(signs.T, BF16),
        jnp.asarray(scale),
        jnp.asarray(coarse, BF16),
    ]
    grad = None
    returned = []
    for number, (span, batches) in enumerate(zip(SPANS, BATCHES)):
        last = number == len(SPANS) - 1
        width = span // ways
        given = tables if last else tables[:5]
        extra = [grad] if last else []
        share = 2 * channels * rows // blocks // LANES
        grad_shape = (ways * blocks, share, LANES) if last else (2 * channels, channels)
        *spread, grad = pl.pallas_call(
            functools.partial(fine_kernel, ways, batches, tiles, last),
            in_specs=[either] * (len(arrived[number]) + len(given) + len(extra)),
            out_specs=[hbm] * (ways + 1 + last),
            out_shape=[pltpu.HBM((rows, width), BF16)] * ways
            + [pltpu.HBM(grad_shape, BF16 if last else F32)]
            + [pltpu.HBM((rows, LANES), F32)] * last,
            scratch_shapes=[
                pltpu.VMEM((ways, 2 * rows, width + (2 * LANES if last else 0)), BF16),
                pltpu.VMEM((ways, rows, width), BF16),
                pltpu.VMEM((2 * channels, channels), F32),
            ]
            + [pltpu.VMEM(one.shape, one.dtype) for one in given]
            + [
                pltpu.VMEM((rows, LANES), F32),
                pltpu.VMEM(grad_shape, BF16),
            ][: 2 * last]
            + [
                pltpu.SemaphoreType.DMA((8 + ways * len(batches),)),
                pltpu.SemaphoreType.DMA((2 + ways * len(batches),)),
            ],
            compiler_params=scoped(FINE_MIB),
            name="fine_levels",
        )(*(arrived[number] if last else held_in(arrived[number])), *in_hbm(*given, *extra))
        if last:
            adjoint, grad, spread = grad, spread[ways], spread[:ways]
        if HOLD_BACK and not last:
            barred = lax.optimization_barrier((*spread, *arrived[number + 1]))
            spread, arrived[number + 1] = list(barred[:ways]), list(barred[ways:])
        returned.append(
            [spread[0]] + [lax.ppermute(spread[s], "chan", back[s]) for s in range(1, ways)]
        )

    shares = lax.all_to_all(grad, ("chan", "morton"), split_axis=0, concat_axis=0, tiled=True)

    out = None
    for number, (first, span) in enumerate(zip(starts, SPANS)):
        carried = [] if out is None else [out]
        out = pl.pallas_call(
            functools.partial(join_kernel, ways, first),
            in_specs=[either] * (3 + ways) + [hbm] * len(carried),
            out_specs=hbm,
            out_shape=pltpu.HBM((rows, block_len), F32),
            scratch_shapes=[
                pltpu.VMEM((rows, LANES), F32),
                pltpu.VMEM((rows, span), BF16),
                pltpu.VMEM((1, span), jnp.int32),
                pltpu.VMEM((ways, rows, span // ways), BF16),
                pltpu.VMEM((rows, span), F32),
                pltpu.SemaphoreType.DMA((2 + 3 * ways,)),
            ],
            input_output_aliases={3 + ways: 0} if carried else {},
            compiler_params=scoped(JOIN_MIB),
            name="join_leaves",
        )(*in_hbm(cotangent, mask, adjoint), *held_in(returned[number]), *carried)
        if number == HOLD:
            out, shares = lax.optimization_barrier((out, shares))
    grad_weight = pl.pallas_call(
        functools.partial(shares_kernel, leaf_total ** (-0.5)),
        out_shape=jax.ShapeDtypeStruct((2 * channels // blocks, rows), F32),
        compiler_params=scoped(JOIN_MIB),
        name="sum_shares",
    )(shares)
    return (out, grad_weight.T)


def solution(mesh):
    placed = (P("chan", "morton"), P("chan", "morton"), P("morton"), P())
    return jax.shard_map(
        local,
        mesh=mesh,
        in_specs=placed,
        out_specs=(P("chan", "morton"), P("chan", "morton")),
        check_vma=False,
    )
```

```python
import functools

import jax
import jax.numpy as jnp
import numpy as np
from jax import lax
from jax.experimental import pallas as pl
from jax.experimental.pallas import tpu as pltpu
from jax.sharding import PartitionSpec as P

half_root = 0.7071067811865476
inv_root_tau = 0.3989422804014327
TILE = 256
SPANS = (12288, 4096)
BATCHES = ((6, 6), (4,))
LANES = 128
F32 = jnp.float32
BF16 = jnp.bfloat16
MIB = 1024 * 1024
FINE_MIB = 40
JOIN_MIB = 16
CUT_MIB = 16


def gelu_slope(values):
    return (
        0.5 * (1.0 + lax.erf(values * half_root))
        + values * jnp.exp(-0.5 * values * values) * inv_root_tau
    )


def sign_tables(width, first_level):
    detail = np.zeros((width, width), np.float32)
    total = np.zeros((width, width), np.float32)
    scale = np.zeros((width,), np.float32)
    col = 0
    for level in range(1, width.bit_length()):
        span = 1 << level
        for first in range(0, width, span):
            middle = first + span // 2
            detail[first:middle, col] = 1.0
            detail[middle : first + span, col] = -1.0
            total[first : first + span, col] = 1.0
            scale[col] = half_root ** (first_level + level)
            col += 1
    return detail, total, scale


def fine_tables():
    detail, total, scale = sign_tables(TILE, 0)
    signs = np.concatenate([detail, total], axis=1)
    return signs, np.concatenate([scale, scale])[None, :]


def coarse_tables(tiles, blocks):
    tile_level = TILE.bit_length() - 1
    block_level = tile_level + tiles.bit_length() - 1
    detail = np.zeros((LANES, LANES), np.float32)
    total = np.zeros((LANES, LANES), np.float32)
    scale = np.zeros((LANES,), np.float32)
    for first, width, level in ((0, tiles, tile_level), (tiles, blocks, block_level)):
        part = slice(first, first + width)
        detail[part, part], total[part, part], scale[part] = sign_tables(width, level)
    signs = np.concatenate([detail, total], axis=1)
    spread = np.zeros((2 * LANES, 2 * LANES), np.float32)
    for copy in range(2):
        spread[copy * tiles : (copy + 1) * tiles] = signs[:tiles]
        first = LANES + copy * blocks
        spread[first : first + blocks] = signs[tiles : tiles + blocks]
    return spread, signs.T, scale[None, :]


def dot(left, right):
    return jnp.dot(left, right, preferred_element_type=F32)


def dot_last(left, right):
    return lax.dot_general(left, right, (((1,), (1,)), ((), ())), preferred_element_type=F32)


def started(src, dst, sem):
    copy = pltpu.make_async_copy(src, dst, sem)
    copy.start()
    return copy


def in_two(values):
    high = values.astype(BF16).astype(F32)
    return high, values - high


def sums_kernel(ways, press_ref, cot_ref, mask_ref, carry_ref, spread_ref, *refs):
    press_buf, cot_buf, mask_buf, carry_buf, spread_buf, in_sems, out_sems = refs
    rows, block_len = press_buf.shape
    width = block_len // ways
    mask_copy = started(mask_ref, mask_buf, in_sems.at[0])
    runs = [pl.ds(sub * width, width) for sub in range(ways)]
    fetched = []
    for sub, run in enumerate(runs):
        fetched.append(started(cot_ref.at[:, run], cot_buf.at[:, run], in_sems.at[1 + 2 * sub]))
        fetched.append(started(press_ref.at[:, run], press_buf.at[:, run], in_sems.at[2 + 2 * sub]))
    half = LANES // 2
    sums = jnp.zeros((2 * rows, LANES), F32)
    lane = lax.broadcasted_iota(jnp.int32, (2 * rows, LANES), 1)
    ones = jnp.ones((TILE, LANES), BF16)
    mask_copy.wait()
    for sub in range(ways):
        fetched[2 * sub].wait()
        fetched[2 * sub + 1].wait()
        numbers = range(sub * width // TILE, (sub + 1) * width // TILE)
        stacked = []
        for tile in numbers:
            leaves = slice(tile * TILE, (tile + 1) * TILE)
            kept = mask_buf[:, leaves].astype(F32).astype(BF16)
            stacked += [press_buf[:, leaves], cot_buf[:, leaves] * kept]
        found = dot(jnp.concatenate(stacked, axis=0), ones)
        for place, tile in enumerate(numbers):
            mine = found[place * 2 * rows : (place + 1) * 2 * rows, :]
            sums = jnp.where(lane % half == tile, mine, sums)
    upper = lane < half
    block = jnp.sum(jnp.where(upper, sums, 0.0), axis=1, keepdims=True)
    row = jnp.broadcast_to(block, sums.shape).T[:1, :]
    spread_buf[...] = jnp.broadcast_to(row, spread_buf.shape)
    sent = [started(spread_buf, spread_ref, out_sems.at[0])]
    high, rest = in_two(sums)
    carry_buf[...] = jnp.where(upper, high, rest).astype(BF16)
    sent.append(started(carry_buf, carry_ref, out_sems.at[1]))
    for copy in sent:
        copy.wait()


def cut_kernel(ways, first, span, closing, press_ref, cot_ref, mask_ref, *refs):
    if closing:
        carry_ref, above_ref, joined_ref, refs = refs[0], refs[1], refs[2], refs[3:]
    else:
        parts, refs = refs[:ways], refs[ways:]
    press_buf, cot_buf, mask_buf, in_sems, out_sems = refs[-5:]
    rows, width = press_buf.shape[0], span // ways
    own = lax.axis_index("chan")
    mask_copy = started(mask_ref.at[:, pl.ds(first, span)], mask_buf, in_sems.at[0])
    fetched, places = [], []
    for step in range(ways):
        start = pl.multiple_of(lax.rem(own + ways - step, ways) * width, LANES)
        run, place = pl.ds(first + start, width), pl.ds(start, width)
        places.append(place)
        fetched.append(started(cot_ref.at[:, run], cot_buf.at[:, place], in_sems.at[1 + 2 * step]))
        fetched.append(
            started(press_ref.at[:, run], press_buf.at[:, place], in_sems.at[2 + 2 * step])
        )
    sent = []
    if closing:
        carry_buf, above_buf = refs[:2]
        parts = [joined_ref.at[lax.rem(own + ways - step, ways)] for step in range(ways)]
        carried = [
            started(above_ref, above_buf, in_sems.at[1 + 2 * ways]),
            started(carry_ref, carry_buf.at[:, pl.ds(0, LANES)], in_sems.at[2 + 2 * ways]),
        ]
        carried[0].wait()
        outer = list(in_two(above_buf[...]))
        outer.append(jnp.zeros((LANES - 2 * above_buf.shape[0], LANES), F32))
        carry_buf[:, LANES:] = jnp.concatenate(outer, axis=0).T.astype(BF16)
        carried[1].wait()
        for step in range(ways):
            place = parts[step].at[:, pl.ds(width, 2 * LANES)]
            sent.append(started(carry_buf, place, out_sems.at[2 * ways + step]))
    mask_copy.wait()
    for step, place in enumerate(places):
        fetched[2 * step].wait()
        cot_buf[:, place] = cot_buf[:, place] * mask_buf[:, place].astype(F32).astype(BF16)
        dst = parts[step].at[pl.ds(rows, rows), pl.ds(0, width)]
        sent.append(started(cot_buf.at[:, place], dst, out_sems.at[2 * step]))
        fetched[2 * step + 1].wait()
        dst = parts[step].at[pl.ds(0, rows), pl.ds(0, width)]
        sent.append(started(press_buf.at[:, place], dst, out_sems.at[2 * step + 1]))
    for copy in sent:
        copy.wait()


def fine_kernel(ways, batches, tiles, last, *refs):
    own, position = lax.axis_index("chan"), lax.axis_index("morton")
    if last:
        joined_ref, refs = refs[0], refs[1:]
        order = [lax.rem(own + step, ways) for step in range(ways)]
    else:
        parts, refs = refs[:ways], refs[ways:]
    w_ref, wt_ref, signs_ref, back_ref, scale_ref, refs = *refs[:5], refs[5:]
    if last:
        coarse_in, grad_in, refs = refs[0], refs[1], refs[2:]
    outs, grad_out, refs = refs[:ways], refs[ways], refs[ways + 1 :]
    if last:
        adjoint_out, total_ref, out_buf, grad_ref, coarse_ref, earlier_ref, adjoint_ref, sems = refs
        fetched_coarse = started(coarse_in, coarse_ref, sems.at[1])
        fetched_grad = started(grad_in, earlier_ref, sems.at[2])
    else:
        total_ref, out_buf, own_buf, sems = refs
        fetched = started(parts[0], own_buf, sems.at[0])
        parts = (own_buf, *parts[1:])
        grad_ref = total_ref
    channels = w_ref.shape[0]
    rows = channels // ways
    width = out_buf.shape[2]
    starts = [sum(batches[:index]) * TILE for index in range(len(batches))]
    runs = [pl.ds(start, batch * TILE) for start, batch in zip(starts, batches)]

    def part(step, low, lanes):
        if last:
            return joined_ref[order[step], low : low + rows, lanes]
        return parts[step][low : low + rows, lanes]

    if not last:
        fetched.wait()
    scale = scale_ref[:1, :]
    sent = []
    for index, run in enumerate(runs):
        batch = batches[index]
        closing = last and index == len(runs) - 1
        here = [pl.ds(starts[index] + tile * TILE, TILE) for tile in range(batch)]

        def stacked(low):
            return jnp.concatenate(
                [part(step, low, lanes) for lanes in here for step in range(ways)], axis=0
            )

        def side_by_side(values):
            return [values[tile * channels : (tile + 1) * channels] for tile in range(batch)]

        def one_by_one(values):
            return jnp.concatenate(
                [
                    (values[:, tile * TILE : (tile + 1) * TILE] * scale).astype(BF16)
                    for tile in range(batch)
                ],
                axis=0,
            )

        press = stacked(0)
        detail = side_by_side((dot(press, signs_ref[:, :TILE]) * scale).astype(BF16))
        total = side_by_side((dot(press, signs_ref[:, TILE:]) * scale).astype(BF16))
        cot_detail = side_by_side(dot(stacked(rows), signs_ref[:, :TILE]) * scale)
        if closing:
            fetched_coarse.wait()
            carried = pl.ds(width, 2 * LANES)
            tops = [part(step, low, carried) for low in (0, rows) for step in range(ways)]
            found = dot(jnp.concatenate(tops, axis=0), coarse_ref[: 2 * LANES, :])
            coarse_scale = scale_ref[1:2, :LANES]
            detail.append((found[:channels, :LANES] * coarse_scale).astype(BF16))
            total.append((found[:channels, LANES:] * coarse_scale).astype(BF16))
            cot_detail.append(found[channels:, :LANES] * coarse_scale)
        both = jnp.concatenate(
            [jnp.concatenate(detail, axis=1), jnp.concatenate(total, axis=1)], axis=0
        )
        mixed = dot(w_ref[...], both)
        slopes = (jnp.concatenate(cot_detail, axis=1) * gelu_slope(mixed)).astype(BF16)
        up = dot(wt_ref[:channels, :], slopes)
        level = dot(wt_ref[channels:, :], slopes)
        nodes = jnp.concatenate([one_by_one(up), one_by_one(level)], axis=1)
        spread = dot(nodes, back_ref[...]).astype(BF16)
        for tile, lanes in enumerate(here):
            out_buf[:, :, lanes] = spread[tile * channels : (tile + 1) * channels].reshape(
                ways, rows, TILE
            )
        for step in range(ways):
            sent.append(
                started(
                    out_buf.at[step, :, run],
                    outs[step].at[:, run],
                    sems.at[3 + index * ways + step],
                )
            )
        if closing:
            coarse = batch * TILE
            nodes = jnp.concatenate(
                [
                    (values[:rows, coarse:] * coarse_scale).astype(BF16)
                    for values in (up, level)
                ],
                axis=1,
            )
            back = jnp.concatenate(
                [coarse_ref[2 * LANES : 3 * LANES, :], coarse_ref[3 * LANES :, :]], axis=0
            )[:, :LANES]
            adjoint = dot(nodes, back)
            lane = lax.broadcasted_iota(jnp.int32, adjoint.shape, 1)
            above = jnp.where(lane == tiles + position, adjoint, 0.0)
            adjoint_ref[...] = adjoint + jnp.sum(above, axis=1, keepdims=True)
            sent.append(started(adjoint_ref, adjoint_out, sems.at[1]))
            counted = jnp.where(position == 0, LANES, tiles)
            counted = jnp.where(own == 0, counted, 0)
            lane = lax.broadcasted_iota(jnp.int32, (channels, LANES), 1)
            shown = jnp.where(lane < counted, slopes[:, coarse:].astype(F32), 0.0).astype(BF16)
            slopes = jnp.concatenate([slopes[:, :coarse], shown], axis=1)
        if last and index == 0:
            fetched_grad.wait()
        found = dot_last(both, slopes)
        if index:
            found = found + total_ref[...]
        elif last:
            found = found + earlier_ref[...]
        total_ref[...] = found
    if last:
        blocks = grad_ref.shape[0] // ways
        cols = 2 * channels // blocks
        for half in range(2):
            for step in range(ways):
                first = half * channels + step * rows
                group = half * channels + lax.rem(own + step, ways) * rows
                for other in range(ways):
                    share = total_ref[first : first + rows, other * rows : (other + 1) * rows]
                    share = share.reshape(rows // cols, 2, cols // 2, rows)
                    share = jnp.concatenate([share[:, 0], share[:, 1]], axis=2)
                    place = lax.rem(own + other, ways) * blocks + group // cols
                    grad_ref[pl.ds(place, rows // cols)] = share.astype(BF16)
    sent.append(started(grad_ref, grad_out, sems.at[0]))
    for copy in sent:
        copy.wait()


def sum_shares(factor, shares_ref, out_ref):
    total = jnp.sum(shares_ref[...].astype(F32), axis=0)
    half = total.shape[1] // 2
    out_ref[...] = jnp.concatenate([total[:, :half], total[:, half:]], axis=0) * factor


def join_kernel(ways, first, factor, cot_ref, mask_ref, adjoint_in, *refs):
    parts = refs[:ways]
    if factor is None:
        out_ref, refs = refs[ways], refs[ways + 1 :]
    else:
        shares_ref, out_ref, grad_out, grad_buf, refs = refs[ways], *refs[ways + 2 : ways + 5], refs[ways + 5 :]
    adjoint_ref, cot_buf, mask_buf, own_buf, out_buf, sems = refs
    width = parts[0].shape[1]
    span = ways * width
    own = lax.axis_index("chan")
    opening = [
        started(mask_ref.at[:, pl.ds(first, span)], mask_buf, sems.at[0]),
        started(parts[0], own_buf, sems.at[1]),
        started(adjoint_in, adjoint_ref, sems.at[2]),
    ]
    parts = (own_buf, *parts[1:])
    places, fetched = [], []
    for step in range(ways):
        start = pl.multiple_of(lax.rem(own + ways - step, ways) * width, TILE)
        places.append(start)
        fetched.append(
            started(
                cot_ref.at[:, pl.ds(first + start, width)],
                cot_buf.at[:, pl.ds(start, width)],
                sems.at[3 + step],
            )
        )
    sent = []
    if factor is not None:
        sum_shares(factor, shares_ref, grad_buf)
        sent.append(started(grad_buf, grad_out, sems.at[3 + 2 * ways]))
    for copy in opening:
        copy.wait()
    lane = lax.broadcasted_iota(jnp.int32, adjoint_ref.shape, 1)
    for step, start in enumerate(places):
        fetched[step].wait()
        for tile in range(width // TILE):
            number = (first + start) // TILE + tile
            above = jnp.sum(
                jnp.where(lane == number, adjoint_ref[...], 0.0), axis=1, keepdims=True
            )
            lanes = pl.ds(pl.multiple_of(start + tile * TILE, TILE), TILE)
            kept = mask_buf[:, lanes].astype(F32)
            out_buf[:, lanes] = (
                cot_buf[:, lanes].astype(F32) * kept
                + parts[step][:, tile * TILE : (tile + 1) * TILE].astype(F32)
                + above
            )
        sent.append(
            started(
                out_buf.at[:, pl.ds(start, width)],
                out_ref.at[:, pl.ds(first + start, width)],
                sems.at[3 + ways + step],
            )
        )
    for copy in sent:
        copy.wait()


def vmem():
    return pl.BlockSpec(memory_space=pltpu.VMEM)


def in_hbm(*arrays):
    return [pltpu.with_memory_space_constraint(array, pltpu.HBM) for array in arrays]


def held_in(parts):
    return in_hbm(parts[0]) + parts[1:]


def scoped(mib):
    return pltpu.CompilerParams(vmem_limit_bytes=mib * MIB)


def local(pressure, cotangent, fluid_mask, weight):
    rows, block_len = pressure.shape
    channels = weight.shape[0]
    ways = lax.axis_size("chan")
    blocks = lax.axis_size("morton")
    tiles = block_len // TILE
    leaf_total = block_len * blocks
    own = lax.axis_index("chan")
    mask = fluid_mask.reshape(1, block_len)
    there = [[(i, (i - step) % ways) for i in range(ways)] for step in range(ways)]
    back = [[(i, (i + step) % ways) for i in range(ways)] for step in range(ways)]
    starts = [sum(SPANS[:number]) for number in range(len(SPANS))]
    hbm = pl.BlockSpec(memory_space=pltpu.HBM)

    def cut(number, *carried):
        first, span = starts[number], SPANS[number]
        width = span // ways + (2 * LANES if carried else 0)
        parts = pl.pallas_call(
            functools.partial(cut_kernel, ways, first, span, bool(carried)),
            in_specs=[hbm] * (3 + len(carried)),
            out_specs=[hbm] * (1 if carried else ways),
            out_shape=[pltpu.HBM((ways, 2 * rows, width), BF16)]
            if carried
            else [pltpu.HBM((2 * rows, width), BF16)] * ways,
            scratch_shapes=[
                pltpu.VMEM((2 * rows, 2 * LANES), BF16),
                pltpu.VMEM((blocks, LANES), F32),
            ][: len(carried)]
            + [
                pltpu.VMEM((rows, span), BF16),
                pltpu.VMEM((rows, span), BF16),
                pltpu.VMEM((1, span), jnp.int32),
                pltpu.SemaphoreType.DMA((3 + 2 * ways,)),
                pltpu.SemaphoreType.DMA((3 * ways,)),
            ],
            compiler_params=scoped(CUT_MIB),
            name="cut_leaves",
        )(*in_hbm(pressure, cotangent, mask, *carried))
        if carried:
            return [lax.all_to_all(parts[0], "chan", split_axis=0, concat_axis=0, tiled=True)]
        return [parts[0]] + [lax.ppermute(parts[s], "chan", there[s]) for s in range(1, ways)]

    arrived = [cut(0)]
    carry, block_sums = pl.pallas_call(
        functools.partial(sums_kernel, ways),
        in_specs=[hbm] * 3,
        out_specs=[hbm] * 2,
        out_shape=[pltpu.HBM((2 * rows, LANES), BF16), pltpu.HBM((blocks, LANES), F32)],
        scratch_shapes=[
            pltpu.VMEM((rows, block_len), BF16),
            pltpu.VMEM((rows, block_len), BF16),
            pltpu.VMEM((1, block_len), jnp.int32),
            pltpu.VMEM((2 * rows, LANES), BF16),
            pltpu.VMEM((blocks, LANES), F32),
            pltpu.SemaphoreType.DMA((1 + 2 * ways,)),
            pltpu.SemaphoreType.DMA((2,)),
        ],
        compiler_params=scoped(CUT_MIB),
        name="sum_tiles",
    )(*in_hbm(pressure, cotangent, mask))
    block_sums = lax.all_to_all(block_sums, "morton", split_axis=0, concat_axis=0, tiled=True)
    arrived.append(cut(1, carry, block_sums))

    turn = own * rows
    mix = lax.dynamic_slice_in_dim(jnp.concatenate([weight, weight], 0), turn, channels, 0)
    mix = jnp.concatenate(
        [
            lax.dynamic_slice_in_dim(jnp.concatenate([half, half], 1), turn, channels, 1)
            for half in (mix[:, :channels], mix[:, channels:])
        ],
        axis=1,
    )
    signs, fine_scale = fine_tables()
    coarse, coarse_back, coarse_scale = coarse_tables(tiles, blocks)
    scale = np.zeros((8, TILE), np.float32)
    scale[0] = fine_scale[0, :TILE]
    scale[1, :LANES] = coarse_scale[0]
    coarse = np.concatenate([coarse, np.pad(coarse_back, ((0, 0), (0, LANES)))], axis=0)
    tables = [
        mix,
        mix.T,
        jnp.asarray(signs, BF16),
        jnp.asarray(signs.T, BF16),
        jnp.asarray(scale),
        jnp.asarray(coarse, BF16),
    ]
    grad = None
    returned = []
    for number, (span, batches) in enumerate(zip(SPANS, BATCHES)):
        last = number == len(SPANS) - 1
        width = span // ways
        extra = in_hbm(tables[5], grad) if last else []
        share = 2 * channels * rows // blocks // LANES
        *spread, grad = pl.pallas_call(
            functools.partial(fine_kernel, ways, batches, tiles, last),
            in_specs=([vmem()] if last else [hbm] + [vmem()] * (ways - 1))
            + [vmem()] * 5
            + [hbm] * len(extra),
            out_specs=[hbm] * (ways + 1 + last),
            out_shape=[pltpu.HBM((rows, width), BF16)] * ways
            + (
                [pltpu.HBM((ways * blocks, share, LANES), BF16), pltpu.HBM((rows, LANES), F32)]
                if last
                else [pltpu.HBM((2 * channels, channels), F32)]
            ),
            scratch_shapes=[
                pltpu.VMEM((2 * channels, channels), F32),
                pltpu.VMEM((ways, rows, width), BF16),
            ]
            + (
                [
                    pltpu.VMEM((ways * blocks, share, LANES), BF16),
                    pltpu.VMEM(tables[5].shape, BF16),
                    pltpu.VMEM((2 * channels, channels), F32),
                    pltpu.VMEM((rows, LANES), F32),
                ]
                if last
                else [pltpu.VMEM((2 * rows, width), BF16)]
            )
            + [pltpu.SemaphoreType.DMA((3 + ways * len(batches),))],
            compiler_params=scoped(FINE_MIB),
            name="fine_levels",
        )(*(arrived[number] if last else held_in(arrived[number])), *tables[:5], *extra)
        if last:
            adjoint, grad, spread = grad, spread[ways], spread[:ways]
        returned.append(
            [spread[0]] + [lax.ppermute(spread[s], "chan", back[s]) for s in range(1, ways)]
        )

    shares = lax.all_to_all(grad, ("chan", "morton"), split_axis=0, concat_axis=0, tiled=True)

    out = None
    for number, (first, span) in enumerate(zip(starts, SPANS)):
        last = number == len(SPANS) - 1
        found = pl.pallas_call(
            functools.partial(join_kernel, ways, first, leaf_total ** (-0.5) if last else None),
            in_specs=[hbm] * 4 + [vmem()] * (ways - 1) + [vmem(), hbm] * last,
            out_specs=[hbm] * (1 + last),
            out_shape=[jax.ShapeDtypeStruct((rows, block_len), F32)]
            + [pltpu.HBM((2 * channels // blocks, rows), F32)] * last,
            scratch_shapes=[pltpu.VMEM((2 * channels // blocks, rows), F32)] * last
            + [
                pltpu.VMEM((rows, LANES), F32),
                pltpu.VMEM((rows, span), BF16),
                pltpu.VMEM((1, span), jnp.int32),
                pltpu.VMEM((rows, span // ways), BF16),
                pltpu.VMEM((rows, span), F32),
                pltpu.SemaphoreType.DMA((4 + 2 * ways,)),
            ],
            input_output_aliases={4 + ways: 0} if last else {},
            compiler_params=scoped(JOIN_MIB),
            name="join_leaves",
        )(
            *in_hbm(cotangent, mask, adjoint),
            *held_in(returned[number]),
            *([shares, out] if last else []),
        )
        out = found[0]
    return (out, found[1].T)


def solution(mesh):
    placed = (P("chan", "morton"), P("chan", "morton"), P("morton"), P())
    return jax.shard_map(
        local,
        mesh=mesh,
        in_specs=placed,
        out_specs=(P("chan", "morton"), P("chan", "morton")),
        check_vma=False,
    )
```

```python
import functools

import jax
import jax.numpy as jnp
import numpy as np
from jax import lax
from jax.experimental import pallas as pl
from jax.experimental.pallas import tpu as pltpu
from jax.sharding import PartitionSpec as P

half_root = 0.7071067811865476
inv_root_tau = 0.3989422804014327
TILE = 256
SPANS = (12288, 4096)
BATCHES = ((6, 6), (4,))
LANES = 128
F32 = jnp.float32
BF16 = jnp.bfloat16
MIB = 1024 * 1024
FINE_MIB = 40
JOIN_MIB = 16
CUT_MIB = 16


def gelu_slope(values):
    return (
        0.5 * (1.0 + lax.erf(values * half_root))
        + values * jnp.exp(-0.5 * values * values) * inv_root_tau
    )


def sign_tables(width, first_level):
    detail = np.zeros((width, width), np.float32)
    total = np.zeros((width, width), np.float32)
    scale = np.zeros((width,), np.float32)
    col = 0
    for level in range(1, width.bit_length()):
        span = 1 << level
        for first in range(0, width, span):
            middle = first + span // 2
            detail[first:middle, col] = 1.0
            detail[middle : first + span, col] = -1.0
            total[first : first + span, col] = 1.0
            scale[col] = half_root ** (first_level + level)
            col += 1
    return detail, total, scale


def fine_tables():
    detail, total, scale = sign_tables(TILE, 0)
    signs = np.concatenate([detail, total], axis=1)
    return signs, np.concatenate([scale, scale])[None, :]


def coarse_tables(tiles, blocks):
    tile_level = TILE.bit_length() - 1
    block_level = tile_level + tiles.bit_length() - 1
    detail = np.zeros((LANES, LANES), np.float32)
    total = np.zeros((LANES, LANES), np.float32)
    scale = np.zeros((LANES,), np.float32)
    for first, width, level in ((0, tiles, tile_level), (tiles, blocks, block_level)):
        part = slice(first, first + width)
        detail[part, part], total[part, part], scale[part] = sign_tables(width, level)
    signs = np.concatenate([detail, total], axis=1)
    spread = np.zeros((2 * LANES, 2 * LANES), np.float32)
    for copy in range(2):
        spread[copy * tiles : (copy + 1) * tiles] = signs[:tiles]
        first = LANES + copy * blocks
        spread[first : first + blocks] = signs[tiles : tiles + blocks]
    return spread, signs.T, scale[None, :]


def dot(left, right):
    return jnp.dot(left, right, preferred_element_type=F32)


def dot_last(left, right):
    return lax.dot_general(left, right, (((1,), (1,)), ((), ())), preferred_element_type=F32)


def started(src, dst, sem):
    copy = pltpu.make_async_copy(src, dst, sem)
    copy.start()
    return copy


def in_two(values):
    high = values.astype(BF16).astype(F32)
    return high, values - high


def sums_kernel(ways, press_ref, cot_ref, mask_ref, carry_ref, spread_ref, *refs):
    press_buf, cot_buf, mask_buf, carry_buf, spread_buf, in_sems, out_sems = refs
    rows, block_len = press_buf.shape
    width = block_len // ways
    mask_copy = started(mask_ref, mask_buf, in_sems.at[0])
    runs = [pl.ds(sub * width, width) for sub in range(ways)]
    fetched = []
    for sub, run in enumerate(runs):
        fetched.append(started(cot_ref.at[:, run], cot_buf.at[:, run], in_sems.at[1 + 2 * sub]))
        fetched.append(started(press_ref.at[:, run], press_buf.at[:, run], in_sems.at[2 + 2 * sub]))
    half = LANES // 2
    sums = jnp.zeros((2 * rows, LANES), F32)
    lane = lax.broadcasted_iota(jnp.int32, (2 * rows, LANES), 1)
    ones = jnp.ones((TILE, LANES), BF16)
    mask_copy.wait()
    for sub in range(ways):
        fetched[2 * sub].wait()
        fetched[2 * sub + 1].wait()
        numbers = range(sub * width // TILE, (sub + 1) * width // TILE)
        stacked = []
        for tile in numbers:
            leaves = slice(tile * TILE, (tile + 1) * TILE)
            kept = mask_buf[:, leaves].astype(F32).astype(BF16)
            stacked += [press_buf[:, leaves], cot_buf[:, leaves] * kept]
        found = dot(jnp.concatenate(stacked, axis=0), ones)
        for place, tile in enumerate(numbers):
            mine = found[place * 2 * rows : (place + 1) * 2 * rows, :]
            sums = jnp.where(lane % half == tile, mine, sums)
    upper = lane < half
    block = jnp.sum(jnp.where(upper, sums, 0.0), axis=1, keepdims=True)
    row = jnp.broadcast_to(block, sums.shape).T[:1, :]
    spread_buf[...] = jnp.broadcast_to(row, spread_buf.shape)
    sent = [started(spread_buf, spread_ref, out_sems.at[0])]
    high, rest = in_two(sums)
    carry_buf[...] = jnp.where(upper, high, rest).astype(BF16)
    sent.append(started(carry_buf, carry_ref, out_sems.at[1]))
    for copy in sent:
        copy.wait()


def cut_kernel(ways, first, span, closing, press_ref, cot_ref, mask_ref, *refs):
    if closing:
        carry_ref, above_ref, joined_ref, refs = refs[0], refs[1], refs[2], refs[3:]
    else:
        parts, refs = refs[:ways], refs[ways:]
    press_buf, cot_buf, mask_buf, in_sems, out_sems = refs[-5:]
    rows, width = press_buf.shape[0], span // ways
    own = lax.axis_index("chan")
    mask_copy = started(mask_ref.at[:, pl.ds(first, span)], mask_buf, in_sems.at[0])
    fetched, places = [], []
    for step in range(ways):
        start = pl.multiple_of(lax.rem(own + ways - step, ways) * width, LANES)
        run, place = pl.ds(first + start, width), pl.ds(start, width)
        places.append(place)
        fetched.append(started(cot_ref.at[:, run], cot_buf.at[:, place], in_sems.at[1 + 2 * step]))
        fetched.append(
            started(press_ref.at[:, run], press_buf.at[:, place], in_sems.at[2 + 2 * step])
        )
    sent = []
    if closing:
        carry_buf, above_buf = refs[:2]
        parts = [joined_ref.at[lax.rem(own + ways - step, ways)] for step in range(ways)]
        carried = [
            started(above_ref, above_buf, in_sems.at[1 + 2 * ways]),
            started(carry_ref, carry_buf.at[:, pl.ds(0, LANES)], in_sems.at[2 + 2 * ways]),
        ]
        carried[0].wait()
        outer = list(in_two(above_buf[...]))
        outer.append(jnp.zeros((LANES - 2 * above_buf.shape[0], LANES), F32))
        carry_buf[:, LANES:] = jnp.concatenate(outer, axis=0).T.astype(BF16)
        carried[1].wait()
        for step in range(ways):
            place = parts[step].at[:, pl.ds(width, 2 * LANES)]
            sent.append(started(carry_buf, place, out_sems.at[2 * ways + step]))
    mask_copy.wait()
    for step, place in enumerate(places):
        fetched[2 * step].wait()
        cot_buf[:, place] = cot_buf[:, place] * mask_buf[:, place].astype(F32).astype(BF16)
        dst = parts[step].at[pl.ds(rows, rows), pl.ds(0, width)]
        sent.append(started(cot_buf.at[:, place], dst, out_sems.at[2 * step]))
        fetched[2 * step + 1].wait()
        dst = parts[step].at[pl.ds(0, rows), pl.ds(0, width)]
        sent.append(started(press_buf.at[:, place], dst, out_sems.at[2 * step + 1]))
    for copy in sent:
        copy.wait()


def fine_kernel(ways, batches, tiles, last, *refs):
    own, position = lax.axis_index("chan"), lax.axis_index("morton")
    if last:
        joined_ref, refs = refs[0], refs[1:]
        order = [lax.rem(own + step, ways) for step in range(ways)]
    else:
        parts, refs = refs[:ways], refs[ways:]
    w_ref, wt_ref, signs_ref, back_ref, scale_ref, refs = *refs[:5], refs[5:]
    if last:
        coarse_in, grad_in, refs = refs[0], refs[1], refs[2:]
    outs, grad_out, refs = refs[:ways], refs[ways], refs[ways + 1 :]
    if last:
        adjoint_out, total_ref, out_buf, grad_ref, coarse_ref, earlier_ref, adjoint_ref, sems = refs
        fetched_coarse = started(coarse_in, coarse_ref, sems.at[1])
        fetched_grad = started(grad_in, earlier_ref, sems.at[2])
    else:
        total_ref, out_buf, own_buf, sems = refs
        fetched = started(parts[0], own_buf, sems.at[0])
        parts = (own_buf, *parts[1:])
        grad_ref = total_ref
    channels = w_ref.shape[0]
    rows = channels // ways
    width = out_buf.shape[2]
    starts = [sum(batches[:index]) * TILE for index in range(len(batches))]
    runs = [pl.ds(start, batch * TILE) for start, batch in zip(starts, batches)]

    def part(step, low, lanes):
        if last:
            return joined_ref[order[step], low : low + rows, lanes]
        return parts[step][low : low + rows, lanes]

    if not last:
        fetched.wait()
    scale = scale_ref[:1, :]
    sent = []
    for index, run in enumerate(runs):
        batch = batches[index]
        closing = last and index == len(runs) - 1
        here = [pl.ds(starts[index] + tile * TILE, TILE) for tile in range(batch)]

        def stacked(low):
            return jnp.concatenate(
                [part(step, low, lanes) for lanes in here for step in range(ways)], axis=0
            )

        def side_by_side(values):
            return [values[tile * channels : (tile + 1) * channels] for tile in range(batch)]

        def one_by_one(values):
            return jnp.concatenate(
                [
                    (values[:, tile * TILE : (tile + 1) * TILE] * scale).astype(BF16)
                    for tile in range(batch)
                ],
                axis=0,
            )

        press = stacked(0)
        detail = side_by_side((dot(press, signs_ref[:, :TILE]) * scale).astype(BF16))
        total = side_by_side((dot(press, signs_ref[:, TILE:]) * scale).astype(BF16))
        cot_detail = side_by_side(dot(stacked(rows), signs_ref[:, :TILE]) * scale)
        if closing:
            fetched_coarse.wait()
            carried = pl.ds(width, 2 * LANES)
            tops = [part(step, low, carried) for low in (0, rows) for step in range(ways)]
            found = dot(jnp.concatenate(tops, axis=0), coarse_ref[: 2 * LANES, :])
            coarse_scale = scale_ref[1:2, :LANES]
            detail.append((found[:channels, :LANES] * coarse_scale).astype(BF16))
            total.append((found[:channels, LANES:] * coarse_scale).astype(BF16))
            cot_detail.append(found[channels:, :LANES] * coarse_scale)
        both = jnp.concatenate(
            [jnp.concatenate(detail, axis=1), jnp.concatenate(total, axis=1)], axis=0
        )
        mixed = dot(w_ref[...], both)
        slopes = (jnp.concatenate(cot_detail, axis=1) * gelu_slope(mixed)).astype(BF16)
        up = dot(wt_ref[:channels, :], slopes)
        level = dot(wt_ref[channels:, :], slopes)
        nodes = jnp.concatenate([one_by_one(up), one_by_one(level)], axis=1)
        spread = dot(nodes, back_ref[...]).astype(BF16)
        for tile, lanes in enumerate(here):
            out_buf[:, :, lanes] = spread[tile * channels : (tile + 1) * channels].reshape(
                ways, rows, TILE
            )
        for step in range(ways):
            sent.append(
                started(
                    out_buf.at[step, :, run],
                    outs[step].at[:, run],
                    sems.at[3 + index * ways + step],
                )
            )
        if closing:
            coarse = batch * TILE
            nodes = jnp.concatenate(
                [
                    (values[:rows, coarse:] * coarse_scale).astype(BF16)
                    for values in (up, level)
                ],
                axis=1,
            )
            back = jnp.concatenate(
                [coarse_ref[2 * LANES : 3 * LANES, :], coarse_ref[3 * LANES :, :]], axis=0
            )[:, :LANES]
            adjoint = dot(nodes, back)
            lane = lax.broadcasted_iota(jnp.int32, adjoint.shape, 1)
            above = jnp.where(lane == tiles + position, adjoint, 0.0)
            adjoint_ref[...] = adjoint + jnp.sum(above, axis=1, keepdims=True)
            sent.append(started(adjoint_ref, adjoint_out, sems.at[1]))
            counted = jnp.where(position == 0, LANES, tiles)
            counted = jnp.where(own == 0, counted, 0)
            lane = lax.broadcasted_iota(jnp.int32, (channels, LANES), 1)
            shown = jnp.where(lane < counted, slopes[:, coarse:].astype(F32), 0.0).astype(BF16)
            slopes = jnp.concatenate([slopes[:, :coarse], shown], axis=1)
        if last and index == 0:
            fetched_grad.wait()
        found = dot_last(both, slopes)
        if index:
            found = found + total_ref[...]
        elif last:
            found = found + earlier_ref[...]
        total_ref[...] = found
    if last:
        blocks = grad_ref.shape[0] // ways
        cols = 2 * channels // blocks
        for half in range(2):
            for step in range(ways):
                first = half * channels + step * rows
                group = half * channels + lax.rem(own + step, ways) * rows
                for other in range(ways):
                    share = total_ref[first : first + rows, other * rows : (other + 1) * rows]
                    share = share.reshape(rows // cols, 2, cols // 2, rows)
                    share = jnp.concatenate([share[:, 0], share[:, 1]], axis=2)
                    place = lax.rem(own + other, ways) * blocks + group // cols
                    grad_ref[pl.ds(place, rows // cols)] = share.astype(BF16)
    sent.append(started(grad_ref, grad_out, sems.at[0]))
    for copy in sent:
        copy.wait()


def join_kernel(ways, span, cot_ref, mask_ref, adjoint_in, *refs):
    parts = refs[:ways]
    out_ref, base_ref, adjoint_ref, cot_buf, mask_buf, own_buf, out_buf, sems = refs[ways:]
    block_len = cot_buf.shape[1]
    width = span // ways
    own = lax.axis_index("chan")
    opening = [
        started(mask_ref, mask_buf, sems.at[0]),
        started(parts[0], own_buf, sems.at[1]),
        started(adjoint_in, adjoint_ref, sems.at[2]),
    ]
    parts = (own_buf, *parts[1:])
    fetched = [started(cot_ref.at[:, pl.ds(0, span)], cot_buf.at[:, pl.ds(0, span)], sems.at[3])]
    rest = pl.ds(span, block_len - span)
    fetched.append(started(cot_ref.at[:, rest], cot_buf.at[:, rest], sems.at[4]))
    for copy in opening:
        copy.wait()
    fetched[0].wait()
    lane = lax.broadcasted_iota(jnp.int32, adjoint_ref.shape, 1)
    sent = []
    for step in range(ways):
        start = pl.multiple_of(lax.rem(own + ways - step, ways) * width, TILE)
        for tile in range(width // TILE):
            above = jnp.sum(
                jnp.where(lane == start // TILE + tile, adjoint_ref[...], 0.0), axis=1, keepdims=True
            )
            lanes = pl.ds(pl.multiple_of(start + tile * TILE, TILE), TILE)
            kept = mask_buf[:, lanes].astype(F32)
            out_buf[:, lanes] = (
                cot_buf[:, lanes].astype(F32) * kept
                + parts[step][:, tile * TILE : (tile + 1) * TILE].astype(F32)
                + above
            )
        place = pl.ds(start, width)
        sent.append(started(out_buf.at[:, place], out_ref.at[:, place], sems.at[5 + step]))
    fetched[1].wait()
    for tile in range(span // TILE, block_len // TILE):
        lanes = slice(tile * TILE, (tile + 1) * TILE)
        kept = mask_buf[:, lanes].astype(F32)
        base_ref[:, tile * TILE - span : (tile + 1) * TILE - span] = (
            cot_buf[:, lanes].astype(F32) * kept + adjoint_ref[:, tile : tile + 1]
        )
    for copy in sent:
        copy.wait()


def last_join_kernel(ways, first, factor, base_ref, *refs):
    parts, shares_ref, refs = refs[:ways], refs[ways], refs[ways + 2 :]
    out_ref, grad_out, grad_buf, own_buf, out_buf, sems = refs
    fetched = started(parts[0], own_buf, sems.at[0])
    parts = (own_buf, *parts[1:])
    width = own_buf.shape[1]
    own = lax.axis_index("chan")
    sent = []
    for step in (*range(1, ways), 0):
        start = pl.multiple_of(lax.rem(own + ways - step, ways) * width, TILE)
        place = pl.ds(start, width)
        if step == 0:
            fetched.wait()
        out_buf[:, place] = base_ref[:, place] + parts[step][...].astype(F32)
        target = out_ref.at[:, pl.ds(pl.multiple_of(first + start, TILE), width)]
        sent.append(started(out_buf.at[:, place], target, sems.at[2 + step]))
    total = jnp.sum(shares_ref[...].astype(F32), axis=0)
    half = total.shape[1] // 2
    grad_buf[...] = jnp.concatenate([total[:, :half], total[:, half:]], axis=0) * factor
    sent.append(started(grad_buf, grad_out, sems.at[1]))
    for copy in sent:
        copy.wait()


def vmem():
    return pl.BlockSpec(memory_space=pltpu.VMEM)


def in_hbm(*arrays):
    return [pltpu.with_memory_space_constraint(array, pltpu.HBM) for array in arrays]


def held_in(parts):
    return in_hbm(parts[0]) + parts[1:]


def scoped(mib):
    return pltpu.CompilerParams(vmem_limit_bytes=mib * MIB)


def local(pressure, cotangent, fluid_mask, weight):
    rows, block_len = pressure.shape
    channels = weight.shape[0]
    ways = lax.axis_size("chan")
    blocks = lax.axis_size("morton")
    tiles = block_len // TILE
    leaf_total = block_len * blocks
    own = lax.axis_index("chan")
    mask = fluid_mask.reshape(1, block_len)
    there = [[(i, (i - step) % ways) for i in range(ways)] for step in range(ways)]
    back = [[(i, (i + step) % ways) for i in range(ways)] for step in range(ways)]
    starts = [sum(SPANS[:number]) for number in range(len(SPANS))]
    hbm = pl.BlockSpec(memory_space=pltpu.HBM)

    def cut(number, *carried):
        first, span = starts[number], SPANS[number]
        width = span // ways + (2 * LANES if carried else 0)
        parts = pl.pallas_call(
            functools.partial(cut_kernel, ways, first, span, bool(carried)),
            in_specs=[hbm] * (3 + len(carried)),
            out_specs=[hbm] * (1 if carried else ways),
            out_shape=[pltpu.HBM((ways, 2 * rows, width), BF16)]
            if carried
            else [pltpu.HBM((2 * rows, width), BF16)] * ways,
            scratch_shapes=[
                pltpu.VMEM((2 * rows, 2 * LANES), BF16),
                pltpu.VMEM((blocks, LANES), F32),
            ][: len(carried)]
            + [
                pltpu.VMEM((rows, span), BF16),
                pltpu.VMEM((rows, span), BF16),
                pltpu.VMEM((1, span), jnp.int32),
                pltpu.SemaphoreType.DMA((3 + 2 * ways,)),
                pltpu.SemaphoreType.DMA((3 * ways,)),
            ],
            compiler_params=scoped(CUT_MIB),
            name="cut_leaves",
        )(*in_hbm(pressure, cotangent, mask, *carried))
        if carried:
            return [lax.all_to_all(parts[0], "chan", split_axis=0, concat_axis=0, tiled=True)]
        return [parts[0]] + [lax.ppermute(parts[s], "chan", there[s]) for s in range(1, ways)]

    arrived = [cut(0)]
    carry, block_sums = pl.pallas_call(
        functools.partial(sums_kernel, ways),
        in_specs=[hbm] * 3,
        out_specs=[hbm] * 2,
        out_shape=[pltpu.HBM((2 * rows, LANES), BF16), pltpu.HBM((blocks, LANES), F32)],
        scratch_shapes=[
            pltpu.VMEM((rows, block_len), BF16),
            pltpu.VMEM((rows, block_len), BF16),
            pltpu.VMEM((1, block_len), jnp.int32),
            pltpu.VMEM((2 * rows, LANES), BF16),
            pltpu.VMEM((blocks, LANES), F32),
            pltpu.SemaphoreType.DMA((1 + 2 * ways,)),
            pltpu.SemaphoreType.DMA((2,)),
        ],
        compiler_params=scoped(CUT_MIB),
        name="sum_tiles",
    )(*in_hbm(pressure, cotangent, mask))
    block_sums = lax.all_to_all(block_sums, "morton", split_axis=0, concat_axis=0, tiled=True)
    arrived.append(cut(1, carry, block_sums))

    turn = own * rows
    mix = lax.dynamic_slice_in_dim(jnp.concatenate([weight, weight], 0), turn, channels, 0)
    mix = jnp.concatenate(
        [
            lax.dynamic_slice_in_dim(jnp.concatenate([half, half], 1), turn, channels, 1)
            for half in (mix[:, :channels], mix[:, channels:])
        ],
        axis=1,
    )
    signs, fine_scale = fine_tables()
    coarse, coarse_back, coarse_scale = coarse_tables(tiles, blocks)
    scale = np.zeros((8, TILE), np.float32)
    scale[0] = fine_scale[0, :TILE]
    scale[1, :LANES] = coarse_scale[0]
    coarse = np.concatenate([coarse, np.pad(coarse_back, ((0, 0), (0, LANES)))], axis=0)
    tables = [
        mix,
        mix.T,
        jnp.asarray(signs, BF16),
        jnp.asarray(signs.T, BF16),
        jnp.asarray(scale),
        jnp.asarray(coarse, BF16),
    ]
    grad = None
    returned = []
    for number, (span, batches) in enumerate(zip(SPANS, BATCHES)):
        last = number == len(SPANS) - 1
        width = span // ways
        extra = in_hbm(tables[5], grad) if last else []
        share = 2 * channels * rows // blocks // LANES
        *spread, grad = pl.pallas_call(
            functools.partial(fine_kernel, ways, batches, tiles, last),
            in_specs=([vmem()] if last else [hbm] + [vmem()] * (ways - 1))
            + [vmem()] * 5
            + [hbm] * len(extra),
            out_specs=[hbm] * (ways + 1 + last),
            out_shape=[pltpu.HBM((rows, width), BF16)] * ways
            + (
                [pltpu.HBM((ways * blocks, share, LANES), BF16), pltpu.HBM((rows, LANES), F32)]
                if last
                else [pltpu.HBM((2 * channels, channels), F32)]
            ),
            scratch_shapes=[
                pltpu.VMEM((2 * channels, channels), F32),
                pltpu.VMEM((ways, rows, width), BF16),
            ]
            + (
                [
                    pltpu.VMEM((ways * blocks, share, LANES), BF16),
                    pltpu.VMEM(tables[5].shape, BF16),
                    pltpu.VMEM((2 * channels, channels), F32),
                    pltpu.VMEM((rows, LANES), F32),
                ]
                if last
                else [pltpu.VMEM((2 * rows, width), BF16)]
            )
            + [pltpu.SemaphoreType.DMA((3 + ways * len(batches),))],
            compiler_params=scoped(FINE_MIB),
            name="fine_levels",
        )(*(arrived[number] if last else held_in(arrived[number])), *tables[:5], *extra)
        if last:
            adjoint, grad, spread = grad, spread[ways], spread[:ways]
        returned.append(
            [spread[0]] + [lax.ppermute(spread[s], "chan", back[s]) for s in range(1, ways)]
        )

    shares = lax.all_to_all(grad, ("chan", "morton"), split_axis=0, concat_axis=0, tiled=True)

    span, rest = SPANS
    out, base = pl.pallas_call(
        functools.partial(join_kernel, ways, span),
        in_specs=[hbm] * 4 + [vmem()] * (ways - 1),
        out_specs=[hbm, vmem()],
        out_shape=[jax.ShapeDtypeStruct((rows, block_len), F32), jax.ShapeDtypeStruct((rows, rest), F32)],
        scratch_shapes=[
            pltpu.VMEM((rows, LANES), F32),
            pltpu.VMEM((rows, block_len), BF16),
            pltpu.VMEM((1, block_len), jnp.int32),
            pltpu.VMEM((rows, span // ways), BF16),
            pltpu.VMEM((rows, span), F32),
            pltpu.SemaphoreType.DMA((5 + ways,)),
        ],
        compiler_params=scoped(JOIN_MIB),
        name="join_leaves",
    )(*in_hbm(cotangent, mask, adjoint), *held_in(returned[0]))
    grad_shape = (2 * channels // blocks, rows)
    out, grad_weight = pl.pallas_call(
        functools.partial(last_join_kernel, ways, span, leaf_total ** (-0.5)),
        in_specs=[vmem(), hbm] + [vmem()] * ways + [hbm],
        out_specs=[hbm] * 2,
        out_shape=[jax.ShapeDtypeStruct((rows, block_len), F32), pltpu.HBM(grad_shape, F32)],
        scratch_shapes=[
            pltpu.VMEM(grad_shape, F32),
            pltpu.VMEM((rows, rest // ways), BF16),
            pltpu.VMEM((rows, rest), F32),
            pltpu.SemaphoreType.DMA((2 + ways,)),
        ],
        input_output_aliases={2 + ways: 0},
        compiler_params=scoped(JOIN_MIB),
        name="join_leaves",
    )(base, *held_in(returned[1]), shares, out)
    return (out, grad_weight.T)


def solution(mesh):
    placed = (P("chan", "morton"), P("chan", "morton"), P("morton"), P())
    return jax.shard_map(
        local,
        mesh=mesh,
        in_specs=placed,
        out_specs=(P("chan", "morton"), P("chan", "morton")),
        check_vma=False,
    )
```

```python
import functools

import jax
import jax.numpy as jnp
import numpy as np
from jax import lax
from jax.experimental import pallas as pl
from jax.experimental.pallas import tpu as pltpu
from jax.sharding import PartitionSpec as P

half_root = 0.7071067811865476
inv_root_tau = 0.3989422804014327
TILE = 256
SPANS = (12288, 4096)
BATCHES = ((6, 6), (4,))
LANES = 128
F32 = jnp.float32
BF16 = jnp.bfloat16
MIB = 1024 * 1024
FINE_MIB = 40
JOIN_MIB = 16
CUT_MIB = 16
ORDER = ((1, 2, 3), (0,))


def gelu_slope(values):
    return (
        0.5 * (1.0 + lax.erf(values * half_root))
        + values * jnp.exp(-0.5 * values * values) * inv_root_tau
    )


def sign_tables(width, first_level):
    detail = np.zeros((width, width), np.float32)
    total = np.zeros((width, width), np.float32)
    scale = np.zeros((width,), np.float32)
    col = 0
    for level in range(1, width.bit_length()):
        span = 1 << level
        for first in range(0, width, span):
            middle = first + span // 2
            detail[first:middle, col] = 1.0
            detail[middle : first + span, col] = -1.0
            total[first : first + span, col] = 1.0
            scale[col] = half_root ** (first_level + level)
            col += 1
    return detail, total, scale


def fine_tables():
    detail, total, scale = sign_tables(TILE, 0)
    signs = np.concatenate([detail, total], axis=1)
    return signs, np.concatenate([scale, scale])[None, :]


def coarse_tables(tiles, blocks):
    tile_level = TILE.bit_length() - 1
    block_level = tile_level + tiles.bit_length() - 1
    detail = np.zeros((LANES, LANES), np.float32)
    total = np.zeros((LANES, LANES), np.float32)
    scale = np.zeros((LANES,), np.float32)
    for first, width, level in ((0, tiles, tile_level), (tiles, blocks, block_level)):
        part = slice(first, first + width)
        detail[part, part], total[part, part], scale[part] = sign_tables(width, level)
    signs = np.concatenate([detail, total], axis=1)
    spread = np.zeros((2 * LANES, 2 * LANES), np.float32)
    for copy in range(2):
        spread[copy * tiles : (copy + 1) * tiles] = signs[:tiles]
        first = LANES + copy * blocks
        spread[first : first + blocks] = signs[tiles : tiles + blocks]
    return spread, signs.T, scale[None, :]


def dot(left, right):
    return jnp.dot(left, right, preferred_element_type=F32)


def dot_last(left, right):
    return lax.dot_general(left, right, (((1,), (1,)), ((), ())), preferred_element_type=F32)


def started(src, dst, sem):
    copy = pltpu.make_async_copy(src, dst, sem)
    copy.start()
    return copy


def in_two(values):
    high = values.astype(BF16).astype(F32)
    return high, values - high


def sums_kernel(ways, press_ref, cot_ref, mask_ref, carry_ref, spread_ref, *refs):
    press_buf, cot_buf, mask_buf, carry_buf, spread_buf, in_sems, out_sems = refs
    rows, block_len = press_buf.shape
    width = block_len // ways
    mask_copy = started(mask_ref, mask_buf, in_sems.at[0])
    runs = [pl.ds(sub * width, width) for sub in range(ways)]
    fetched = []
    for sub, run in enumerate(runs):
        fetched.append(started(cot_ref.at[:, run], cot_buf.at[:, run], in_sems.at[1 + 2 * sub]))
        fetched.append(started(press_ref.at[:, run], press_buf.at[:, run], in_sems.at[2 + 2 * sub]))
    half = LANES // 2
    sums = jnp.zeros((2 * rows, LANES), F32)
    lane = lax.broadcasted_iota(jnp.int32, (2 * rows, LANES), 1)
    ones = jnp.ones((TILE, LANES), BF16)
    mask_copy.wait()
    for sub in range(ways):
        fetched[2 * sub].wait()
        fetched[2 * sub + 1].wait()
        numbers = range(sub * width // TILE, (sub + 1) * width // TILE)
        stacked = []
        for tile in numbers:
            leaves = slice(tile * TILE, (tile + 1) * TILE)
            kept = mask_buf[:, leaves].astype(F32).astype(BF16)
            stacked += [press_buf[:, leaves], cot_buf[:, leaves] * kept]
        found = dot(jnp.concatenate(stacked, axis=0), ones)
        for place, tile in enumerate(numbers):
            mine = found[place * 2 * rows : (place + 1) * 2 * rows, :]
            sums = jnp.where(lane % half == tile, mine, sums)
    upper = lane < half
    block = jnp.sum(jnp.where(upper, sums, 0.0), axis=1, keepdims=True)
    row = jnp.broadcast_to(block, sums.shape).T[:1, :]
    spread_buf[...] = jnp.broadcast_to(row, spread_buf.shape)
    sent = [started(spread_buf, spread_ref, out_sems.at[0])]
    high, rest = in_two(sums)
    carry_buf[...] = jnp.where(upper, high, rest).astype(BF16)
    sent.append(started(carry_buf, carry_ref, out_sems.at[1]))
    for copy in sent:
        copy.wait()


def cut_kernel(ways, first, span, steps, closing, press_ref, cot_ref, mask_ref, *refs):
    if closing:
        carry_ref, above_ref, joined_ref, refs = refs[0], refs[1], refs[2], refs[3:]
    else:
        parts, refs = dict(zip(steps, refs)), refs[len(steps) :]
    press_buf, cot_buf, mask_buf, in_sems, out_sems = refs[-5:]
    rows, width = press_buf.shape[0], span // ways
    own = lax.axis_index("chan")
    mask_copy = started(mask_ref.at[:, pl.ds(first, span)], mask_buf, in_sems.at[0])
    fetched, places = {}, {}
    for step in steps:
        start = pl.multiple_of(lax.rem(own + ways - step, ways) * width, LANES)
        run, place = pl.ds(first + start, width), pl.ds(start, width)
        places[step] = place
        fetched[step] = (
            started(cot_ref.at[:, run], cot_buf.at[:, place], in_sems.at[1 + 2 * step]),
            started(press_ref.at[:, run], press_buf.at[:, place], in_sems.at[2 + 2 * step]),
        )
    sent = []
    if closing:
        carry_buf, above_buf = refs[:2]
        parts = [joined_ref.at[lax.rem(own + ways - step, ways)] for step in range(ways)]
        carried = [
            started(above_ref, above_buf, in_sems.at[1 + 2 * ways]),
            started(carry_ref, carry_buf.at[:, pl.ds(0, LANES)], in_sems.at[2 + 2 * ways]),
        ]
        carried[0].wait()
        outer = list(in_two(above_buf[...]))
        outer.append(jnp.zeros((LANES - 2 * above_buf.shape[0], LANES), F32))
        carry_buf[:, LANES:] = jnp.concatenate(outer, axis=0).T.astype(BF16)
        carried[1].wait()
        for step in range(ways):
            place = parts[step].at[:, pl.ds(width, 2 * LANES)]
            sent.append(started(carry_buf, place, out_sems.at[2 * ways + step]))
    mask_copy.wait()
    for step, place in places.items():
        fetched[step][0].wait()
        cot_buf[:, place] = cot_buf[:, place] * mask_buf[:, place].astype(F32).astype(BF16)
        dst = parts[step].at[pl.ds(rows, rows), pl.ds(0, width)]
        sent.append(started(cot_buf.at[:, place], dst, out_sems.at[2 * step]))
        fetched[step][1].wait()
        dst = parts[step].at[pl.ds(0, rows), pl.ds(0, width)]
        sent.append(started(press_buf.at[:, place], dst, out_sems.at[2 * step + 1]))
    for copy in sent:
        copy.wait()


def fine_kernel(ways, batches, tiles, last, *refs):
    own, position = lax.axis_index("chan"), lax.axis_index("morton")
    if last:
        joined_ref, refs = refs[0], refs[1:]
        order = [lax.rem(own + step, ways) for step in range(ways)]
    else:
        parts, refs = refs[:ways], refs[ways:]
    w_ref, wt_ref, signs_ref, back_ref, scale_ref, refs = *refs[:5], refs[5:]
    if last:
        coarse_in, grad_in, refs = refs[0], refs[1], refs[2:]
    outs, grad_out, refs = refs[:ways], refs[ways], refs[ways + 1 :]
    if last:
        adjoint_out, total_ref, out_buf, grad_ref, coarse_ref, earlier_ref, adjoint_ref, sems = refs
        fetched_coarse = started(coarse_in, coarse_ref, sems.at[1])
        fetched_grad = started(grad_in, earlier_ref, sems.at[2])
    else:
        total_ref, out_buf, own_buf, sems = refs
        fetched = started(parts[0], own_buf, sems.at[0])
        parts = (own_buf, *parts[1:])
        grad_ref = total_ref
    channels = w_ref.shape[0]
    rows = channels // ways
    width = out_buf.shape[2]
    starts = [sum(batches[:index]) * TILE for index in range(len(batches))]
    runs = [pl.ds(start, batch * TILE) for start, batch in zip(starts, batches)]

    def part(step, low, lanes):
        if last:
            return joined_ref[order[step], low : low + rows, lanes]
        return parts[step][low : low + rows, lanes]

    if not last:
        fetched.wait()
    scale = scale_ref[:1, :]
    sent = []
    for index, run in enumerate(runs):
        batch = batches[index]
        closing = last and index == len(runs) - 1
        here = [pl.ds(starts[index] + tile * TILE, TILE) for tile in range(batch)]

        def stacked(low):
            return jnp.concatenate(
                [part(step, low, lanes) for lanes in here for step in range(ways)], axis=0
            )

        def side_by_side(values):
            return [values[tile * channels : (tile + 1) * channels] for tile in range(batch)]

        def one_by_one(values):
            return jnp.concatenate(
                [
                    (values[:, tile * TILE : (tile + 1) * TILE] * scale).astype(BF16)
                    for tile in range(batch)
                ],
                axis=0,
            )

        press = stacked(0)
        detail = side_by_side((dot(press, signs_ref[:, :TILE]) * scale).astype(BF16))
        total = side_by_side((dot(press, signs_ref[:, TILE:]) * scale).astype(BF16))
        cot_detail = side_by_side(dot(stacked(rows), signs_ref[:, :TILE]) * scale)
        if closing:
            fetched_coarse.wait()
            carried = pl.ds(width, 2 * LANES)
            tops = [part(step, low, carried) for low in (0, rows) for step in range(ways)]
            found = dot(jnp.concatenate(tops, axis=0), coarse_ref[: 2 * LANES, :])
            coarse_scale = scale_ref[1:2, :LANES]
            detail.append((found[:channels, :LANES] * coarse_scale).astype(BF16))
            total.append((found[:channels, LANES:] * coarse_scale).astype(BF16))
            cot_detail.append(found[channels:, :LANES] * coarse_scale)
        both = jnp.concatenate(
            [jnp.concatenate(detail, axis=1), jnp.concatenate(total, axis=1)], axis=0
        )
        mixed = dot(w_ref[...], both)
        slopes = (jnp.concatenate(cot_detail, axis=1) * gelu_slope(mixed)).astype(BF16)
        up = dot(wt_ref[:channels, :], slopes)
        level = dot(wt_ref[channels:, :], slopes)
        nodes = jnp.concatenate([one_by_one(up), one_by_one(level)], axis=1)
        spread = dot(nodes, back_ref[...]).astype(BF16)
        for tile, lanes in enumerate(here):
            out_buf[:, :, lanes] = spread[tile * channels : (tile + 1) * channels].reshape(
                ways, rows, TILE
            )
        for step in range(ways):
            sent.append(
                started(
                    out_buf.at[step, :, run],
                    outs[step].at[:, run],
                    sems.at[3 + index * ways + step],
                )
            )
        if closing:
            coarse = batch * TILE
            nodes = jnp.concatenate(
                [
                    (values[:rows, coarse:] * coarse_scale).astype(BF16)
                    for values in (up, level)
                ],
                axis=1,
            )
            back = jnp.concatenate(
                [coarse_ref[2 * LANES : 3 * LANES, :], coarse_ref[3 * LANES :, :]], axis=0
            )[:, :LANES]
            adjoint = dot(nodes, back)
            lane = lax.broadcasted_iota(jnp.int32, adjoint.shape, 1)
            above = jnp.where(lane == tiles + position, adjoint, 0.0)
            adjoint_ref[...] = adjoint + jnp.sum(above, axis=1, keepdims=True)
            sent.append(started(adjoint_ref, adjoint_out, sems.at[1]))
            counted = jnp.where(position == 0, LANES, tiles)
            counted = jnp.where(own == 0, counted, 0)
            lane = lax.broadcasted_iota(jnp.int32, (channels, LANES), 1)
            shown = jnp.where(lane < counted, slopes[:, coarse:].astype(F32), 0.0).astype(BF16)
            slopes = jnp.concatenate([slopes[:, :coarse], shown], axis=1)
        if last and index == 0:
            fetched_grad.wait()
        found = dot_last(both, slopes)
        if index:
            found = found + total_ref[...]
        elif last:
            found = found + earlier_ref[...]
        total_ref[...] = found
    if last:
        blocks = grad_ref.shape[0] // ways
        cols = 2 * channels // blocks
        for half in range(2):
            for step in range(ways):
                first = half * channels + step * rows
                group = half * channels + lax.rem(own + step, ways) * rows
                for other in range(ways):
                    share = total_ref[first : first + rows, other * rows : (other + 1) * rows]
                    share = share.reshape(rows // cols, 2, cols // 2, rows)
                    share = jnp.concatenate([share[:, 0], share[:, 1]], axis=2)
                    place = lax.rem(own + other, ways) * blocks + group // cols
                    grad_ref[pl.ds(place, rows // cols)] = share.astype(BF16)
    sent.append(started(grad_ref, grad_out, sems.at[0]))
    for copy in sent:
        copy.wait()


def join_kernel(ways, span, cot_ref, mask_ref, adjoint_in, *refs):
    parts = refs[:ways]
    out_ref, base_ref, adjoint_ref, cot_buf, mask_buf, own_buf, out_buf, sems = refs[ways:]
    block_len = cot_buf.shape[1]
    width = span // ways
    own = lax.axis_index("chan")
    opening = [
        started(mask_ref, mask_buf, sems.at[0]),
        started(parts[0], own_buf, sems.at[1]),
        started(adjoint_in, adjoint_ref, sems.at[2]),
    ]
    parts = (own_buf, *parts[1:])
    fetched = [started(cot_ref.at[:, pl.ds(0, span)], cot_buf.at[:, pl.ds(0, span)], sems.at[3])]
    rest = pl.ds(span, block_len - span)
    fetched.append(started(cot_ref.at[:, rest], cot_buf.at[:, rest], sems.at[4]))
    for copy in opening:
        copy.wait()
    fetched[0].wait()
    lane = lax.broadcasted_iota(jnp.int32, adjoint_ref.shape, 1)
    sent = []
    for step in range(ways):
        start = pl.multiple_of(lax.rem(own + ways - step, ways) * width, TILE)
        for tile in range(width // TILE):
            above = jnp.sum(
                jnp.where(lane == start // TILE + tile, adjoint_ref[...], 0.0), axis=1, keepdims=True
            )
            lanes = pl.ds(pl.multiple_of(start + tile * TILE, TILE), TILE)
            kept = mask_buf[:, lanes].astype(F32)
            out_buf[:, lanes] = (
                cot_buf[:, lanes].astype(F32) * kept
                + parts[step][:, tile * TILE : (tile + 1) * TILE].astype(F32)
                + above
            )
        place = pl.ds(start, width)
        sent.append(started(out_buf.at[:, place], out_ref.at[:, place], sems.at[5 + step]))
    fetched[1].wait()
    for tile in range(span // TILE, block_len // TILE):
        lanes = slice(tile * TILE, (tile + 1) * TILE)
        kept = mask_buf[:, lanes].astype(F32)
        base_ref[:, tile * TILE - span : (tile + 1) * TILE - span] = (
            cot_buf[:, lanes].astype(F32) * kept + adjoint_ref[:, tile : tile + 1]
        )
    for copy in sent:
        copy.wait()


def last_join_kernel(ways, first, factor, base_ref, *refs):
    parts, shares_ref, refs = refs[:ways], refs[ways], refs[ways + 2 :]
    out_ref, grad_out, grad_buf, own_buf, out_buf, sems = refs
    fetched = started(parts[0], own_buf, sems.at[0])
    parts = (own_buf, *parts[1:])
    width = own_buf.shape[1]
    own = lax.axis_index("chan")
    sent = []
    for step in (*range(1, ways), 0):
        start = pl.multiple_of(lax.rem(own + ways - step, ways) * width, TILE)
        place = pl.ds(start, width)
        if step == 0:
            fetched.wait()
        out_buf[:, place] = base_ref[:, place] + parts[step][...].astype(F32)
        target = out_ref.at[:, pl.ds(pl.multiple_of(first + start, TILE), width)]
        sent.append(started(out_buf.at[:, place], target, sems.at[2 + step]))
    total = jnp.sum(shares_ref[...].astype(F32), axis=0)
    half = total.shape[1] // 2
    grad_buf[...] = jnp.concatenate([total[:, :half], total[:, half:]], axis=0) * factor
    sent.append(started(grad_buf, grad_out, sems.at[1]))
    for copy in sent:
        copy.wait()


def vmem():
    return pl.BlockSpec(memory_space=pltpu.VMEM)


def in_hbm(*arrays):
    return [pltpu.with_memory_space_constraint(array, pltpu.HBM) for array in arrays]


def held_in(parts):
    return in_hbm(parts[0]) + parts[1:]


def scoped(mib):
    return pltpu.CompilerParams(vmem_limit_bytes=mib * MIB)


def local(pressure, cotangent, fluid_mask, weight):
    rows, block_len = pressure.shape
    channels = weight.shape[0]
    ways = lax.axis_size("chan")
    blocks = lax.axis_size("morton")
    tiles = block_len // TILE
    leaf_total = block_len * blocks
    own = lax.axis_index("chan")
    mask = fluid_mask.reshape(1, block_len)
    there = [[(i, (i - step) % ways) for i in range(ways)] for step in range(ways)]
    back = [[(i, (i + step) % ways) for i in range(ways)] for step in range(ways)]
    starts = [sum(SPANS[:number]) for number in range(len(SPANS))]
    hbm = pl.BlockSpec(memory_space=pltpu.HBM)

    def cut(number, steps, *carried):
        first, span = starts[number], SPANS[number]
        width = span // ways + (2 * LANES if carried else 0)
        parts = pl.pallas_call(
            functools.partial(cut_kernel, ways, first, span, steps, bool(carried)),
            in_specs=[hbm] * (3 + len(carried)),
            out_specs=[hbm] * (1 if carried else len(steps)),
            out_shape=[pltpu.HBM((ways, 2 * rows, width), BF16)]
            if carried
            else [pltpu.HBM((2 * rows, width), BF16)] * len(steps),
            scratch_shapes=[
                pltpu.VMEM((2 * rows, 2 * LANES), BF16),
                pltpu.VMEM((blocks, LANES), F32),
            ][: len(carried)]
            + [
                pltpu.VMEM((rows, span), BF16),
                pltpu.VMEM((rows, span), BF16),
                pltpu.VMEM((1, span), jnp.int32),
                pltpu.SemaphoreType.DMA((3 + 2 * ways,)),
                pltpu.SemaphoreType.DMA((3 * ways,)),
            ],
            compiler_params=scoped(CUT_MIB),
            name="cut_leaves",
        )(*in_hbm(pressure, cotangent, mask, *carried))
        if carried:
            return [lax.all_to_all(parts[0], "chan", split_axis=0, concat_axis=0, tiled=True)]
        return {
            step: lax.ppermute(one, "chan", there[step]) if step else one
            for step, one in zip(steps, parts)
        }

    opened = {}
    for steps in ORDER:
        opened.update(cut(0, steps))
    arrived = [[opened[step] for step in range(ways)]]
    carry, block_sums = pl.pallas_call(
        functools.partial(sums_kernel, ways),
        in_specs=[hbm] * 3,
        out_specs=[hbm] * 2,
        out_shape=[pltpu.HBM((2 * rows, LANES), BF16), pltpu.HBM((blocks, LANES), F32)],
        scratch_shapes=[
            pltpu.VMEM((rows, block_len), BF16),
            pltpu.VMEM((rows, block_len), BF16),
            pltpu.VMEM((1, block_len), jnp.int32),
            pltpu.VMEM((2 * rows, LANES), BF16),
            pltpu.VMEM((blocks, LANES), F32),
            pltpu.SemaphoreType.DMA((1 + 2 * ways,)),
            pltpu.SemaphoreType.DMA((2,)),
        ],
        compiler_params=scoped(CUT_MIB),
        name="sum_tiles",
    )(*in_hbm(pressure, cotangent, mask))
    block_sums = lax.all_to_all(block_sums, "morton", split_axis=0, concat_axis=0, tiled=True)
    arrived.append(cut(1, tuple(range(ways)), carry, block_sums))

    turn = own * rows
    mix = lax.dynamic_slice_in_dim(jnp.concatenate([weight, weight], 0), turn, channels, 0)
    mix = jnp.concatenate(
        [
            lax.dynamic_slice_in_dim(jnp.concatenate([half, half], 1), turn, channels, 1)
            for half in (mix[:, :channels], mix[:, channels:])
        ],
        axis=1,
    )
    signs, fine_scale = fine_tables()
    coarse, coarse_back, coarse_scale = coarse_tables(tiles, blocks)
    scale = np.zeros((8, TILE), np.float32)
    scale[0] = fine_scale[0, :TILE]
    scale[1, :LANES] = coarse_scale[0]
    coarse = np.concatenate([coarse, np.pad(coarse_back, ((0, 0), (0, LANES)))], axis=0)
    tables = [
        mix,
        mix.T,
        jnp.asarray(signs, BF16),
        jnp.asarray(signs.T, BF16),
        jnp.asarray(scale),
        jnp.asarray(coarse, BF16),
    ]
    grad = None
    returned = []
    for number, (span, batches) in enumerate(zip(SPANS, BATCHES)):
        last = number == len(SPANS) - 1
        width = span // ways
        extra = in_hbm(tables[5], grad) if last else []
        share = 2 * channels * rows // blocks // LANES
        *spread, grad = pl.pallas_call(
            functools.partial(fine_kernel, ways, batches, tiles, last),
            in_specs=([vmem()] if last else [hbm] + [vmem()] * (ways - 1))
            + [vmem()] * 5
            + [hbm] * len(extra),
            out_specs=[hbm] * (ways + 1 + last),
            out_shape=[pltpu.HBM((rows, width), BF16)] * ways
            + (
                [pltpu.HBM((ways * blocks, share, LANES), BF16), pltpu.HBM((rows, LANES), F32)]
                if last
                else [pltpu.HBM((2 * channels, channels), F32)]
            ),
            scratch_shapes=[
                pltpu.VMEM((2 * channels, channels), F32),
                pltpu.VMEM((ways, rows, width), BF16),
            ]
            + (
                [
                    pltpu.VMEM((ways * blocks, share, LANES), BF16),
                    pltpu.VMEM(tables[5].shape, BF16),
                    pltpu.VMEM((2 * channels, channels), F32),
                    pltpu.VMEM((rows, LANES), F32),
                ]
                if last
                else [pltpu.VMEM((2 * rows, width), BF16)]
            )
            + [pltpu.SemaphoreType.DMA((3 + ways * len(batches),))],
            compiler_params=scoped(FINE_MIB),
            name="fine_levels",
        )(*(arrived[number] if last else held_in(arrived[number])), *tables[:5], *extra)
        if last:
            adjoint, grad, spread = grad, spread[ways], spread[:ways]
        returned.append(
            [spread[0]] + [lax.ppermute(spread[s], "chan", back[s]) for s in range(1, ways)]
        )

    shares = lax.all_to_all(grad, ("chan", "morton"), split_axis=0, concat_axis=0, tiled=True)

    span, rest = SPANS
    out, base = pl.pallas_call(
        functools.partial(join_kernel, ways, span),
        in_specs=[hbm] * 4 + [vmem()] * (ways - 1),
        out_specs=[hbm, vmem()],
        out_shape=[jax.ShapeDtypeStruct((rows, block_len), F32), jax.ShapeDtypeStruct((rows, rest), F32)],
        scratch_shapes=[
            pltpu.VMEM((rows, LANES), F32),
            pltpu.VMEM((rows, block_len), BF16),
            pltpu.VMEM((1, block_len), jnp.int32),
            pltpu.VMEM((rows, span // ways), BF16),
            pltpu.VMEM((rows, span), F32),
            pltpu.SemaphoreType.DMA((5 + ways,)),
        ],
        compiler_params=scoped(JOIN_MIB),
        name="join_leaves",
    )(*in_hbm(cotangent, mask, adjoint), *held_in(returned[0]))
    grad_shape = (2 * channels // blocks, rows)
    out, grad_weight = pl.pallas_call(
        functools.partial(last_join_kernel, ways, span, leaf_total ** (-0.5)),
        in_specs=[vmem(), hbm] + [vmem()] * ways + [hbm],
        out_specs=[hbm] * 2,
        out_shape=[jax.ShapeDtypeStruct((rows, block_len), F32), pltpu.HBM(grad_shape, F32)],
        scratch_shapes=[
            pltpu.VMEM(grad_shape, F32),
            pltpu.VMEM((rows, rest // ways), BF16),
            pltpu.VMEM((rows, rest), F32),
            pltpu.SemaphoreType.DMA((2 + ways,)),
        ],
        input_output_aliases={2 + ways: 0},
        compiler_params=scoped(JOIN_MIB),
        name="join_leaves",
    )(base, *held_in(returned[1]), shares, out)
    return (out, grad_weight.T)


def solution(mesh):
    placed = (P("chan", "morton"), P("chan", "morton"), P("morton"), P())
    return jax.shard_map(
        local,
        mesh=mesh,
        in_specs=placed,
        out_specs=(P("chan", "morton"), P("chan", "morton")),
        check_vma=False,
    )
```

```python
import functools

import jax
import jax.numpy as jnp
import numpy as np
from jax import lax
from jax.experimental import pallas as pl
from jax.experimental.pallas import tpu as pltpu
from jax.sharding import PartitionSpec as P

half_root = 0.7071067811865476
inv_root_tau = 0.3989422804014327
TILE = 256
SPANS = (12288, 4096)
BATCHES = ((6, 6), (4,))
LANES = 128
F32 = jnp.float32
BF16 = jnp.bfloat16
MIB = 1024 * 1024
FINE_MIB = 40
JOIN_MIB = 16
CUT_MIB = 16
ORDER = ((1, 2, 3), (0,))


def gelu_slope(values):
    return (
        0.5 * (1.0 + lax.erf(values * half_root))
        + values * jnp.exp(-0.5 * values * values) * inv_root_tau
    )


def sign_tables(width, first_level):
    detail = np.zeros((width, width), np.float32)
    total = np.zeros((width, width), np.float32)
    scale = np.zeros((width,), np.float32)
    col = 0
    for level in range(1, width.bit_length()):
        span = 1 << level
        for first in range(0, width, span):
            middle = first + span // 2
            detail[first:middle, col] = 1.0
            detail[middle : first + span, col] = -1.0
            total[first : first + span, col] = 1.0
            scale[col] = half_root ** (first_level + level)
            col += 1
    return detail, total, scale


def fine_tables():
    detail, total, scale = sign_tables(TILE, 0)
    signs = np.concatenate([detail, total], axis=1)
    return signs, np.concatenate([scale, scale])[None, :]


def coarse_tables(tiles, blocks):
    tile_level = TILE.bit_length() - 1
    block_level = tile_level + tiles.bit_length() - 1
    detail = np.zeros((LANES, LANES), np.float32)
    total = np.zeros((LANES, LANES), np.float32)
    scale = np.zeros((LANES,), np.float32)
    for first, width, level in ((0, tiles, tile_level), (tiles, blocks, block_level)):
        part = slice(first, first + width)
        detail[part, part], total[part, part], scale[part] = sign_tables(width, level)
    signs = np.concatenate([detail, total], axis=1)
    spread = np.zeros((2 * LANES, 2 * LANES), np.float32)
    for copy in range(2):
        spread[copy * tiles : (copy + 1) * tiles] = signs[:tiles]
        first = LANES + copy * blocks
        spread[first : first + blocks] = signs[tiles : tiles + blocks]
    return spread, signs.T, scale[None, :]


def dot(left, right):
    return jnp.dot(left, right, preferred_element_type=F32)


def dot_last(left, right):
    return lax.dot_general(left, right, (((1,), (1,)), ((), ())), preferred_element_type=F32)


def started(src, dst, sem):
    copy = pltpu.make_async_copy(src, dst, sem)
    copy.start()
    return copy


def in_two(values):
    high = values.astype(BF16).astype(F32)
    return high, values - high


def sums_kernel(ways, press_ref, cot_ref, mask_ref, carry_ref, spread_ref, *refs):
    press_buf, cot_buf, mask_buf, carry_buf, spread_buf, in_sems, out_sems = refs
    rows, block_len = press_buf.shape
    width = block_len // ways
    mask_copy = started(mask_ref, mask_buf, in_sems.at[0])
    runs = [pl.ds(sub * width, width) for sub in range(ways)]
    fetched = []
    for sub, run in enumerate(runs):
        fetched.append(started(cot_ref.at[:, run], cot_buf.at[:, run], in_sems.at[1 + 2 * sub]))
        fetched.append(started(press_ref.at[:, run], press_buf.at[:, run], in_sems.at[2 + 2 * sub]))
    half = LANES // 2
    sums = jnp.zeros((2 * rows, LANES), F32)
    lane = lax.broadcasted_iota(jnp.int32, (2 * rows, LANES), 1)
    ones = jnp.ones((TILE, LANES), BF16)
    mask_copy.wait()
    for sub in range(ways):
        fetched[2 * sub].wait()
        fetched[2 * sub + 1].wait()
        numbers = range(sub * width // TILE, (sub + 1) * width // TILE)
        stacked = []
        for tile in numbers:
            leaves = slice(tile * TILE, (tile + 1) * TILE)
            kept = mask_buf[:, leaves].astype(F32).astype(BF16)
            stacked += [press_buf[:, leaves], cot_buf[:, leaves] * kept]
        found = dot(jnp.concatenate(stacked, axis=0), ones)
        for place, tile in enumerate(numbers):
            mine = found[place * 2 * rows : (place + 1) * 2 * rows, :]
            sums = jnp.where(lane % half == tile, mine, sums)
    upper = lane < half
    block = jnp.sum(jnp.where(upper, sums, 0.0), axis=1, keepdims=True)
    row = jnp.broadcast_to(block, sums.shape).T[:1, :]
    spread_buf[...] = jnp.broadcast_to(row, spread_buf.shape)
    sent = [started(spread_buf, spread_ref, out_sems.at[0])]
    high, rest = in_two(sums)
    carry_buf[...] = jnp.where(upper, high, rest).astype(BF16)
    sent.append(started(carry_buf, carry_ref, out_sems.at[1]))
    for copy in sent:
        copy.wait()


def cut_kernel(ways, first, span, steps, closing, press_ref, cot_ref, mask_ref, *refs):
    if closing:
        carry_ref, above_ref, joined_ref, refs = refs[0], refs[1], refs[2], refs[3:]
    else:
        parts, refs = dict(zip(steps, refs)), refs[len(steps) :]
    press_buf, cot_buf, mask_buf, in_sems, out_sems = refs[-5:]
    rows, width = press_buf.shape[0], span // ways
    own = lax.axis_index("chan")
    mask_copy = started(mask_ref.at[:, pl.ds(first, span)], mask_buf, in_sems.at[0])
    fetched, places = {}, {}
    for step in steps:
        start = pl.multiple_of(lax.rem(own + ways - step, ways) * width, LANES)
        run, place = pl.ds(first + start, width), pl.ds(start, width)
        places[step] = place
        fetched[step] = (
            started(cot_ref.at[:, run], cot_buf.at[:, place], in_sems.at[1 + 2 * step]),
            started(press_ref.at[:, run], press_buf.at[:, place], in_sems.at[2 + 2 * step]),
        )
    sent = []
    if closing:
        carry_buf, above_buf = refs[:2]
        parts = [joined_ref.at[lax.rem(own + ways - step, ways)] for step in range(ways)]
        carried = [
            started(above_ref, above_buf, in_sems.at[1 + 2 * ways]),
            started(carry_ref, carry_buf.at[:, pl.ds(0, LANES)], in_sems.at[2 + 2 * ways]),
        ]
        carried[0].wait()
        outer = list(in_two(above_buf[...]))
        outer.append(jnp.zeros((LANES - 2 * above_buf.shape[0], LANES), F32))
        carry_buf[:, LANES:] = jnp.concatenate(outer, axis=0).T.astype(BF16)
        carried[1].wait()
        for step in range(ways):
            place = parts[step].at[:, pl.ds(width, 2 * LANES)]
            sent.append(started(carry_buf, place, out_sems.at[2 * ways + step]))
    mask_copy.wait()
    for step, place in places.items():
        fetched[step][1].wait()
        dst = parts[step].at[pl.ds(0, rows), pl.ds(0, width)]
        sent.append(started(press_buf.at[:, place], dst, out_sems.at[2 * step + 1]))
        fetched[step][0].wait()
        cot_buf[:, place] = cot_buf[:, place] * mask_buf[:, place].astype(F32).astype(BF16)
        dst = parts[step].at[pl.ds(rows, rows), pl.ds(0, width)]
        sent.append(started(cot_buf.at[:, place], dst, out_sems.at[2 * step]))
    for copy in sent:
        copy.wait()


def fine_kernel(ways, batches, tiles, last, *refs):
    own, position = lax.axis_index("chan"), lax.axis_index("morton")
    if last:
        joined_ref, refs = refs[0], refs[1:]
        order = [lax.rem(own + step, ways) for step in range(ways)]
    else:
        parts, refs = refs[:ways], refs[ways:]
    w_ref, wt_ref, signs_ref, back_ref, scale_ref, refs = *refs[:5], refs[5:]
    if last:
        coarse_in, grad_in, refs = refs[0], refs[1], refs[2:]
    outs, grad_out, refs = refs[:ways], refs[ways], refs[ways + 1 :]
    if last:
        adjoint_out, total_ref, out_buf, grad_ref, coarse_ref, earlier_ref, adjoint_ref, sems = refs
        fetched_coarse = started(coarse_in, coarse_ref, sems.at[1])
        fetched_grad = started(grad_in, earlier_ref, sems.at[2])
    else:
        total_ref, out_buf, own_buf, sems = refs
        fetched = started(parts[0], own_buf, sems.at[0])
        parts = (own_buf, *parts[1:])
        grad_ref = total_ref
    channels = w_ref.shape[0]
    rows = channels // ways
    width = out_buf.shape[2]
    starts = [sum(batches[:index]) * TILE for index in range(len(batches))]
    runs = [pl.ds(start, batch * TILE) for start, batch in zip(starts, batches)]

    def part(step, low, lanes):
        if last:
            return joined_ref[order[step], low : low + rows, lanes]
        return parts[step][low : low + rows, lanes]

    if not last:
        fetched.wait()
    scale = scale_ref[:1, :]
    sent = []
    for index, run in enumerate(runs):
        batch = batches[index]
        closing = last and index == len(runs) - 1
        here = [pl.ds(starts[index] + tile * TILE, TILE) for tile in range(batch)]

        def stacked(low):
            return jnp.concatenate(
                [part(step, low, lanes) for lanes in here for step in range(ways)], axis=0
            )

        def side_by_side(values):
            return [values[tile * channels : (tile + 1) * channels] for tile in range(batch)]

        def one_by_one(values):
            return jnp.concatenate(
                [
                    (values[:, tile * TILE : (tile + 1) * TILE] * scale).astype(BF16)
                    for tile in range(batch)
                ],
                axis=0,
            )

        press = stacked(0)
        detail = side_by_side((dot(press, signs_ref[:, :TILE]) * scale).astype(BF16))
        total = side_by_side((dot(press, signs_ref[:, TILE:]) * scale).astype(BF16))
        cot_detail = side_by_side(dot(stacked(rows), signs_ref[:, :TILE]) * scale)
        if closing:
            fetched_coarse.wait()
            carried = pl.ds(width, 2 * LANES)
            tops = [part(step, low, carried) for low in (0, rows) for step in range(ways)]
            found = dot(jnp.concatenate(tops, axis=0), coarse_ref[: 2 * LANES, :])
            coarse_scale = scale_ref[1:2, :LANES]
            detail.append((found[:channels, :LANES] * coarse_scale).astype(BF16))
            total.append((found[:channels, LANES:] * coarse_scale).astype(BF16))
            cot_detail.append(found[channels:, :LANES] * coarse_scale)
        both = jnp.concatenate(
            [jnp.concatenate(detail, axis=1), jnp.concatenate(total, axis=1)], axis=0
        )
        mixed = dot(w_ref[...], both)
        slopes = (jnp.concatenate(cot_detail, axis=1) * gelu_slope(mixed)).astype(BF16)
        up = dot(wt_ref[:channels, :], slopes)
        level = dot(wt_ref[channels:, :], slopes)
        nodes = jnp.concatenate([one_by_one(up), one_by_one(level)], axis=1)
        spread = dot(nodes, back_ref[...]).astype(BF16)
        for tile, lanes in enumerate(here):
            out_buf[:, :, lanes] = spread[tile * channels : (tile + 1) * channels].reshape(
                ways, rows, TILE
            )
        for step in range(ways):
            sent.append(
                started(
                    out_buf.at[step, :, run],
                    outs[step].at[:, run],
                    sems.at[3 + index * ways + step],
                )
            )
        if closing:
            coarse = batch * TILE
            nodes = jnp.concatenate(
                [
                    (values[:rows, coarse:] * coarse_scale).astype(BF16)
                    for values in (up, level)
                ],
                axis=1,
            )
            back = jnp.concatenate(
                [coarse_ref[2 * LANES : 3 * LANES, :], coarse_ref[3 * LANES :, :]], axis=0
            )[:, :LANES]
            adjoint = dot(nodes, back)
            lane = lax.broadcasted_iota(jnp.int32, adjoint.shape, 1)
            above = jnp.where(lane == tiles + position, adjoint, 0.0)
            adjoint_ref[...] = adjoint + jnp.sum(above, axis=1, keepdims=True)
            sent.append(started(adjoint_ref, adjoint_out, sems.at[1]))
            counted = jnp.where(position == 0, LANES, tiles)
            counted = jnp.where(own == 0, counted, 0)
            lane = lax.broadcasted_iota(jnp.int32, (channels, LANES), 1)
            shown = jnp.where(lane < counted, slopes[:, coarse:].astype(F32), 0.0).astype(BF16)
            slopes = jnp.concatenate([slopes[:, :coarse], shown], axis=1)
        if last and index == 0:
            fetched_grad.wait()
        found = dot_last(both, slopes)
        if index:
            found = found + total_ref[...]
        elif last:
            found = found + earlier_ref[...]
        total_ref[...] = found
    if last:
        blocks = grad_ref.shape[0] // ways
        cols = 2 * channels // blocks
        for half in range(2):
            for step in range(ways):
                first = half * channels + step * rows
                group = half * channels + lax.rem(own + step, ways) * rows
                for other in range(ways):
                    share = total_ref[first : first + rows, other * rows : (other + 1) * rows]
                    share = share.reshape(rows // cols, 2, cols // 2, rows)
                    share = jnp.concatenate([share[:, 0], share[:, 1]], axis=2)
                    place = lax.rem(own + other, ways) * blocks + group // cols
                    grad_ref[pl.ds(place, rows // cols)] = share.astype(BF16)
    sent.append(started(grad_ref, grad_out, sems.at[0]))
    for copy in sent:
        copy.wait()


def join_kernel(ways, span, cot_ref, mask_ref, adjoint_in, *refs):
    parts = refs[:ways]
    out_ref, base_ref, adjoint_ref, cot_buf, mask_buf, own_buf, out_buf, sems = refs[ways:]
    block_len = cot_buf.shape[1]
    width = span // ways
    own = lax.axis_index("chan")
    opening = [
        started(mask_ref, mask_buf, sems.at[0]),
        started(parts[0], own_buf, sems.at[1]),
        started(adjoint_in, adjoint_ref, sems.at[2]),
    ]
    parts = (own_buf, *parts[1:])
    fetched = [started(cot_ref.at[:, pl.ds(0, span)], cot_buf.at[:, pl.ds(0, span)], sems.at[3])]
    rest = pl.ds(span, block_len - span)
    fetched.append(started(cot_ref.at[:, rest], cot_buf.at[:, rest], sems.at[4]))
    for copy in opening:
        copy.wait()
    fetched[0].wait()
    lane = lax.broadcasted_iota(jnp.int32, adjoint_ref.shape, 1)
    sent = []
    for step in range(ways):
        start = pl.multiple_of(lax.rem(own + ways - step, ways) * width, TILE)
        for tile in range(width // TILE):
            above = jnp.sum(
                jnp.where(lane == start // TILE + tile, adjoint_ref[...], 0.0), axis=1, keepdims=True
            )
            lanes = pl.ds(pl.multiple_of(start + tile * TILE, TILE), TILE)
            kept = mask_buf[:, lanes].astype(F32)
            out_buf[:, lanes] = (
                cot_buf[:, lanes].astype(F32) * kept
                + parts[step][:, tile * TILE : (tile + 1) * TILE].astype(F32)
                + above
            )
        place = pl.ds(start, width)
        sent.append(started(out_buf.at[:, place], out_ref.at[:, place], sems.at[5 + step]))
    fetched[1].wait()
    for tile in range(span // TILE, block_len // TILE):
        lanes = slice(tile * TILE, (tile + 1) * TILE)
        kept = mask_buf[:, lanes].astype(F32)
        base_ref[:, tile * TILE - span : (tile + 1) * TILE - span] = (
            cot_buf[:, lanes].astype(F32) * kept + adjoint_ref[:, tile : tile + 1]
        )
    for copy in sent:
        copy.wait()


def last_join_kernel(ways, first, factor, base_ref, *refs):
    parts, shares_ref, refs = refs[:ways], refs[ways], refs[ways + 2 :]
    out_ref, grad_out, grad_buf, own_buf, out_buf, sems = refs
    fetched = started(parts[0], own_buf, sems.at[0])
    parts = (own_buf, *parts[1:])
    width = own_buf.shape[1]
    own = lax.axis_index("chan")
    sent = []
    for step in (*range(1, ways), 0):
        start = pl.multiple_of(lax.rem(own + ways - step, ways) * width, TILE)
        place = pl.ds(start, width)
        if step == 0:
            fetched.wait()
        out_buf[:, place] = base_ref[:, place] + parts[step][...].astype(F32)
        target = out_ref.at[:, pl.ds(pl.multiple_of(first + start, TILE), width)]
        sent.append(started(out_buf.at[:, place], target, sems.at[2 + step]))
    total = jnp.sum(shares_ref[...].astype(F32), axis=0)
    half = total.shape[1] // 2
    grad_buf[...] = jnp.concatenate([total[:, :half], total[:, half:]], axis=0) * factor
    sent.append(started(grad_buf, grad_out, sems.at[1]))
    for copy in sent:
        copy.wait()


def vmem():
    return pl.BlockSpec(memory_space=pltpu.VMEM)


def in_hbm(*arrays):
    return [pltpu.with_memory_space_constraint(array, pltpu.HBM) for array in arrays]


def held_in(parts):
    return in_hbm(parts[0]) + parts[1:]


def scoped(mib):
    return pltpu.CompilerParams(vmem_limit_bytes=mib * MIB)


def local(pressure, cotangent, fluid_mask, weight):
    rows, block_len = pressure.shape
    channels = weight.shape[0]
    ways = lax.axis_size("chan")
    blocks = lax.axis_size("morton")
    tiles = block_len // TILE
    leaf_total = block_len * blocks
    own = lax.axis_index("chan")
    mask = fluid_mask.reshape(1, block_len)
    there = [[(i, (i - step) % ways) for i in range(ways)] for step in range(ways)]
    back = [[(i, (i + step) % ways) for i in range(ways)] for step in range(ways)]
    starts = [sum(SPANS[:number]) for number in range(len(SPANS))]
    hbm = pl.BlockSpec(memory_space=pltpu.HBM)

    def cut(number, steps, *carried):
        first, span = starts[number], SPANS[number]
        width = span // ways + (2 * LANES if carried else 0)
        parts = pl.pallas_call(
            functools.partial(cut_kernel, ways, first, span, steps, bool(carried)),
            in_specs=[hbm] * (3 + len(carried)),
            out_specs=[hbm] * (1 if carried else len(steps)),
            out_shape=[pltpu.HBM((ways, 2 * rows, width), BF16)]
            if carried
            else [pltpu.HBM((2 * rows, width), BF16)] * len(steps),
            scratch_shapes=[
                pltpu.VMEM((2 * rows, 2 * LANES), BF16),
                pltpu.VMEM((blocks, LANES), F32),
            ][: len(carried)]
            + [
                pltpu.VMEM((rows, span), BF16),
                pltpu.VMEM((rows, span), BF16),
                pltpu.VMEM((1, span), jnp.int32),
                pltpu.SemaphoreType.DMA((3 + 2 * ways,)),
                pltpu.SemaphoreType.DMA((3 * ways,)),
            ],
            compiler_params=scoped(CUT_MIB),
            name="cut_leaves",
        )(*in_hbm(pressure, cotangent, mask, *carried))
        if carried:
            return [lax.all_to_all(parts[0], "chan", split_axis=0, concat_axis=0, tiled=True)]
        return {
            step: lax.ppermute(one, "chan", there[step]) if step else one
            for step, one in zip(steps, parts)
        }

    opened = {}
    for steps in ORDER:
        opened.update(cut(0, steps))
    arrived = [[opened[step] for step in range(ways)]]
    carry, block_sums = pl.pallas_call(
        functools.partial(sums_kernel, ways),
        in_specs=[hbm] * 3,
        out_specs=[hbm] * 2,
        out_shape=[pltpu.HBM((2 * rows, LANES), BF16), pltpu.HBM((blocks, LANES), F32)],
        scratch_shapes=[
            pltpu.VMEM((rows, block_len), BF16),
            pltpu.VMEM((rows, block_len), BF16),
            pltpu.VMEM((1, block_len), jnp.int32),
            pltpu.VMEM((2 * rows, LANES), BF16),
            pltpu.VMEM((blocks, LANES), F32),
            pltpu.SemaphoreType.DMA((1 + 2 * ways,)),
            pltpu.SemaphoreType.DMA((2,)),
        ],
        compiler_params=scoped(CUT_MIB),
        name="sum_tiles",
    )(*in_hbm(pressure, cotangent, mask))
    block_sums = lax.all_to_all(block_sums, "morton", split_axis=0, concat_axis=0, tiled=True)
    arrived.append(cut(1, tuple(range(ways)), carry, block_sums))

    turn = own * rows
    mix = lax.dynamic_slice_in_dim(jnp.concatenate([weight, weight], 0), turn, channels, 0)
    mix = jnp.concatenate(
        [
            lax.dynamic_slice_in_dim(jnp.concatenate([half, half], 1), turn, channels, 1)
            for half in (mix[:, :channels], mix[:, channels:])
        ],
        axis=1,
    )
    signs, fine_scale = fine_tables()
    coarse, coarse_back, coarse_scale = coarse_tables(tiles, blocks)
    scale = np.zeros((8, TILE), np.float32)
    scale[0] = fine_scale[0, :TILE]
    scale[1, :LANES] = coarse_scale[0]
    coarse = np.concatenate([coarse, np.pad(coarse_back, ((0, 0), (0, LANES)))], axis=0)
    tables = [
        mix,
        mix.T,
        jnp.asarray(signs, BF16),
        jnp.asarray(signs.T, BF16),
        jnp.asarray(scale),
        jnp.asarray(coarse, BF16),
    ]
    grad = None
    returned = []
    for number, (span, batches) in enumerate(zip(SPANS, BATCHES)):
        last = number == len(SPANS) - 1
        width = span // ways
        extra = in_hbm(tables[5], grad) if last else []
        share = 2 * channels * rows // blocks // LANES
        *spread, grad = pl.pallas_call(
            functools.partial(fine_kernel, ways, batches, tiles, last),
            in_specs=([vmem()] if last else [hbm] + [vmem()] * (ways - 1))
            + [vmem()] * 5
            + [hbm] * len(extra),
            out_specs=[hbm] * (ways + 1 + last),
            out_shape=[pltpu.HBM((rows, width), BF16)] * ways
            + (
                [pltpu.HBM((ways * blocks, share, LANES), BF16), pltpu.HBM((rows, LANES), F32)]
                if last
                else [pltpu.HBM((2 * channels, channels), F32)]
            ),
            scratch_shapes=[
                pltpu.VMEM((2 * channels, channels), F32),
                pltpu.VMEM((ways, rows, width), BF16),
            ]
            + (
                [
                    pltpu.VMEM((ways * blocks, share, LANES), BF16),
                    pltpu.VMEM(tables[5].shape, BF16),
                    pltpu.VMEM((2 * channels, channels), F32),
                    pltpu.VMEM((rows, LANES), F32),
                ]
                if last
                else [pltpu.VMEM((2 * rows, width), BF16)]
            )
            + [pltpu.SemaphoreType.DMA((3 + ways * len(batches),))],
            compiler_params=scoped(FINE_MIB),
            name="fine_levels",
        )(*(arrived[number] if last else held_in(arrived[number])), *tables[:5], *extra)
        if last:
            adjoint, grad, spread = grad, spread[ways], spread[:ways]
        returned.append(
            [spread[0]] + [lax.ppermute(spread[s], "chan", back[s]) for s in range(1, ways)]
        )

    shares = lax.all_to_all(grad, ("chan", "morton"), split_axis=0, concat_axis=0, tiled=True)

    span, rest = SPANS
    out, base = pl.pallas_call(
        functools.partial(join_kernel, ways, span),
        in_specs=[hbm] * 4 + [vmem()] * (ways - 1),
        out_specs=[hbm, vmem()],
        out_shape=[jax.ShapeDtypeStruct((rows, block_len), F32), jax.ShapeDtypeStruct((rows, rest), F32)],
        scratch_shapes=[
            pltpu.VMEM((rows, LANES), F32),
            pltpu.VMEM((rows, block_len), BF16),
            pltpu.VMEM((1, block_len), jnp.int32),
            pltpu.VMEM((rows, span // ways), BF16),
            pltpu.VMEM((rows, span), F32),
            pltpu.SemaphoreType.DMA((5 + ways,)),
        ],
        compiler_params=scoped(JOIN_MIB),
        name="join_leaves",
    )(*in_hbm(cotangent, mask, adjoint), *held_in(returned[0]))
    grad_shape = (2 * channels // blocks, rows)
    out, grad_weight = pl.pallas_call(
        functools.partial(last_join_kernel, ways, span, leaf_total ** (-0.5)),
        in_specs=[vmem(), hbm] + [vmem()] * ways + [hbm],
        out_specs=[hbm] * 2,
        out_shape=[jax.ShapeDtypeStruct((rows, block_len), F32), pltpu.HBM(grad_shape, F32)],
        scratch_shapes=[
            pltpu.VMEM(grad_shape, F32),
            pltpu.VMEM((rows, rest // ways), BF16),
            pltpu.VMEM((rows, rest), F32),
            pltpu.SemaphoreType.DMA((2 + ways,)),
        ],
        input_output_aliases={2 + ways: 0},
        compiler_params=scoped(JOIN_MIB),
        name="join_leaves",
    )(base, *held_in(returned[1]), shares, out)
    return (out, grad_weight.T)


def solution(mesh):
    placed = (P("chan", "morton"), P("chan", "morton"), P("morton"), P())
    return jax.shard_map(
        local,
        mesh=mesh,
        in_specs=placed,
        out_specs=(P("chan", "morton"), P("chan", "morton")),
        check_vma=False,
    )
```
